32 devices in a mesh: src: 4 (over z), tm: 8 (over y, x, core).
Axes of the slice: x: 2, y: 2, z: 4, core: 2. Of those that a mesh axis runs over, the one named last changes fastest.
Arguments:
- src_design: float32 [4096, 5, 128], P(('src', 'tm')), may hold values from -6 to 6
- att_design: float32 [4096, 3, 128], P(('src', 'tm')), may hold values from -6 to 6
- obs_frac: float32 [4096, 128], P(('src', 'tm')), may hold values from 0 to 1
- obs_knot: int32 [4096, 128], P(('src', 'tm')), may hold values from 0 to 124
- observed: float32 [4096, 128], P(('src', 'tm'))
- tile_slot: int32 [4096], P(('src', 'tm')), may hold values from 0 to 63, as said below
- tile_offset: int32 [4096], P(('src', 'tm')), may hold values from 0 to 4095
- tile_valid: int32 [4096], P(('src', 'tm')), may hold values from 8 to 128, as said below
- slot_block: int32 [256, 8], P(('src', 'tm')), may hold values from 0 to 31, as said below
Outputs:
- src_solution: float32 [1024, 5, 128], P(('src', 'tm'))
- att_solution: float32 [3, 32768], P(None, 'tm')
The draws below stay inside these ranges and needn't reach their ends.
Inputs may be any that keep to these rules, and one draw needn't show every extreme that they name: `slot_block`: each row lists 8 distinct local source blocks. `tile_slot`: every slot of every device is named by at least one of that device's tiles. Rows at or after tile_valid are padding.
All inputs are finite; a program needn't handle non-finite values.
Results may differ from the reference program's by a relative error of at most 0.00026.
Values sent between devices are 32-bit elements; how exact they have to be, the bound alone decides.
No kernel may reach another device: no remote copies, remote signals or barrier semaphores. Data moves between devices by JAX's collectives and lax.ppermute only.
A program may use at most 64 MiB of HBM per device.

```python
import jax
import jax.numpy as jnp

BS = 128
KN = 4096
HW = 128
CAP = 8
SB_DEV = 32
TILES_DEV = 128
ITERS = 2
SBLOCKS = 1024
TILES = 4096
KNOTS = 32768
SLOTS = 64
REQROWS = 256
N_TM = 8


def draw_observed(key, part):
    position = jnp.arange(TILES, dtype=jnp.float32)[:, None] / TILES
    return jax.random.normal(key, (TILES, BS), jnp.float32) * (1.0 + 2.0 * position)


def draw_slot_block(key, part):
    keys = jax.random.split(key, REQROWS)

    def one_row(row_key):
        return jax.random.permutation(row_key, SB_DEV)[:CAP]
    return jax.vmap(one_row)(keys).astype(jnp.int32)


def draw_tile_slot(key, part):
    count = TILES // TILES_DEV
    keys = jax.random.split(key, count)

    def one_device(dev_key):
        first, second = jax.random.split(dev_key)
        covered = jax.random.permutation(first, SLOTS)
        others = jax.random.randint(second, (TILES_DEV - SLOTS,), 0, SLOTS)
        return jnp.concatenate([covered, others]).astype(jnp.int32)
    return jax.vmap(one_device)(keys).reshape(-1).astype(jnp.int32)


def draw_tile_valid(key, part):
    count = TILES // TILES_DEV
    first, second = jax.random.split(key)
    floors = jax.random.randint(first, (count, 1), 8, BS)
    upper = jax.random.randint(second, (count, TILES_DEV), 0, BS + 1)
    value = floors + upper * (BS + 1 - floors) // (BS + 1)
    lane_ids = jnp.arange(TILES_DEV)[None, :]
    value = jnp.where(lane_ids == 0, BS, value)
    value = jnp.where(lane_ids == 1, 8, value)
    return value.reshape(-1).astype(jnp.int32)


def plant(result, key, smallest, top_value):
    index_at = [jax.random.randint(jax.random.fold_in(key, axis), (), 0, length) for axis, length in enumerate(result.shape)]
    widest = result.shape.index(max(result.shape))
    neighbour = index_at[:widest] + [(index_at[widest] + 1) % result.shape[widest]] + index_at[widest + 1:]
    return result.at[tuple(index_at)].set(smallest).at[tuple(neighbour)].set(top_value)


def steps_of(own_key, shape, cuts, low, top_value):
    factor_of = 1.0
    for dim, parts in cuts:
        draws = jax.random.uniform(jax.random.fold_in(jax.random.fold_in(own_key, 6), dim), (parts,), jnp.float32, low / len(cuts), top_value / len(cuts))
        factor_of = factor_of * jnp.repeat(jnp.exp(draws), shape[dim] // parts).reshape((-1,) + (1,) * (len(shape) - 1 - dim))
    return factor_of


def normal_values(key, dims, spread, reach, cuts=(), held_as=jnp.bfloat16):
    array = spread * jax.random.normal(key, dims, jnp.float32)
    if cuts:
        array = array * steps_of(key, dims, cuts, -0.22, 0.18)
    return jnp.clip(array, -reach, reach).astype(held_as)


def setup_inputs(seed: int = 0) -> dict:
    seeds = jax.random.split(jax.random.key(seed), 10)
    return {
        "src_design": normal_values(seeds[0], (TILES, 5, BS), 1.0, 6.0, ((0, 32),), jnp.float32),
        "att_design": normal_values(seeds[1], (TILES, 3, BS), 1.0, 6.0, ((0, 32),), jnp.float32),
        "obs_frac": jnp.clip(1.0 * jax.random.uniform(seeds[2], (TILES, BS), jnp.float32) ** steps_of(seeds[2], (TILES, BS), ((0, 32),), -0.2, 0.2), 0.0, 1.0),
        "obs_knot": plant(jax.random.randint(seeds[3], (TILES, BS), 0, HW - 3), jax.random.fold_in(seeds[3], 1), 0, (HW - 3) - 1).astype(jnp.int32),
        "observed": draw_observed(jax.random.fold_in(seeds[9], 71), 0),
        "tile_slot": draw_tile_slot(jax.random.fold_in(seeds[9], 71), 0),
        "tile_offset": plant(jax.random.randint(seeds[6], (TILES,), 0, KN), jax.random.fold_in(seeds[6], 1), 0, KN - 1).astype(jnp.int32),
        "tile_valid": draw_tile_valid(jax.random.fold_in(seeds[9], 71), 0),
        "slot_block": draw_slot_block(jax.random.fold_in(seeds[9], 71), 0),
    }


def spline_weights(fraction):
    remain = 1.0 - fraction
    square = fraction * fraction
    cubed = square * fraction
    return (remain * remain * remain / 6.0, (3.0 * cubed - 6.0 * square + 4.0) / 6.0, (-3.0 * cubed + 3.0 * square + 3.0 * fraction + 1.0) / 6.0, cubed / 6.0)


def reference(src_design, att_design, obs_frac, obs_knot, observed, tile_slot, tile_offset, tile_valid, slot_block):
    tile_ids = jnp.arange(TILES, dtype=jnp.int32)
    device = tile_ids // TILES_DEV
    time_block = device % N_TM
    group = device - time_block
    owner = tile_slot // CAP
    local_block = slot_block[device * N_TM + owner, tile_slot % CAP]
    block = ((group + owner) * SB_DEV + local_block).astype(jnp.int32)
    lane_ids = jnp.arange(BS, dtype=jnp.int32)
    valid_rows = (lane_ids[None, :] < tile_valid[:, None]).astype(jnp.float32)
    knot_base = (time_block * KN + tile_offset)[:, None] + obs_knot
    weights = spline_weights(obs_frac)
    knot_index = jnp.concatenate([(knot_base + order).reshape(-1) for order in range(4)]).astype(jnp.int32)

    def forward(dir_src, dir_att):
        extended = jnp.concatenate([dir_att, jnp.zeros((3, HW), jnp.float32)], axis=1)
        predicted = jnp.sum(src_design * dir_src[block], axis=1)
        for axis_id in range(3):
            picked = extended[axis_id][knot_index].reshape(4, TILES, BS)
            spline = weights[0] * picked[0] + weights[1] * picked[1] + weights[2] * picked[2] + weights[3] * picked[3]
            predicted = predicted + att_design[:, axis_id, :] * spline
        return valid_rows * predicted

    def adjoint(resid):
        src_term = jax.ops.segment_sum(src_design * resid[:, None, :], block, num_segments=SBLOCKS)
        per_axis = []
        for axis_id in range(3):
            scaled = att_design[:, axis_id, :] * resid
            weighted = jnp.concatenate([(weights[order] * scaled).reshape(-1) for order in range(4)])
            per_axis.append(jax.ops.segment_sum(weighted, knot_index, num_segments=KNOTS + HW)[:KNOTS])
        return src_term, jnp.stack(per_axis)

    def operator(vector):
        image = adjoint(forward(vector[0], vector[1]))
        return (image[0] + 1.0 * vector[0], image[1] + 1.0 * vector[1])

    def inner(left, right):
        return jnp.sum(left[0] * right[0]) + jnp.sum(left[1] * right[1])

    solution = (jnp.zeros((SBLOCKS, 5, BS), jnp.float32), jnp.zeros((3, KNOTS), jnp.float32))
    residual = adjoint(valid_rows * observed)
    direction = residual
    norm_now = inner(residual, residual)
    for step in range(ITERS):
        image = operator(direction)
        step_len = norm_now / inner(direction, image)
        solution = (solution[0] + step_len * direction[0], solution[1] + step_len * direction[1])
        residual = (residual[0] - step_len * image[0], residual[1] - step_len * image[1])
        if step + 1 < ITERS:
            norm_next = inner(residual, residual)
            ratio = norm_next / norm_now
            direction = (residual[0] + ratio * direction[0], residual[1] + ratio * direction[1])
            norm_now = norm_next
    return (solution[0], solution[1])
```

```python
import functools

import jax
import jax.numpy as jnp
from jax import lax
from jax.experimental import pallas as pl
from jax.experimental.pallas import tpu as pltpu
from jax.sharding import PartitionSpec as P

KN = 4096
HW = 128
SB_DEV = 32
damping = 1.0

LANES = 128
ROWS = KN // LANES
ROWS_PAD = (ROWS + 8) // 8 * 8
AXES = 3
PARAMS = 5
CAP = 8
EXTRA = PARAMS * CAP
PIECE = EXTRA + 8
UNROLL = 4
F32 = jnp.float32
BF16 = jnp.bfloat16


def iota(shape, dim):
    return lax.broadcasted_iota(jnp.int32, shape, dim)


def spline_weights(fraction):
    remain = 1.0 - fraction
    square = fraction * fraction
    cubed = square * fraction
    return (
        remain * remain * remain / 6.0,
        (3.0 * cubed - 6.0 * square + 4.0) / 6.0,
        (-3.0 * cubed + 3.0 * square + 3.0 * fraction + 1.0) / 6.0,
        cubed / 6.0,
    )


def split2(value):
    high = value.astype(BF16)
    return high, (value - high.astype(F32)).astype(BF16)


def split3(value):
    high, rest = value.astype(BF16), None
    rest = value - high.astype(F32)
    middle = rest.astype(BF16)
    return high, middle, (rest - middle.astype(F32)).astype(BF16)


def total(value):
    return jnp.sum(jnp.sum(value, axis=0, keepdims=True), axis=1, keepdims=True)


def row_of(ref, row):
    return jnp.broadcast_to(ref[pl.ds(row, 1), :], (8, LANES))


def add_adjoint(tiles, values, design, slot_ref, offset_ref, knot_ref, acc, knots):
    lane_row = iota((LANES, LANES), 0).astype(F32)
    outs = []
    for t, resid in zip(tiles, values):
        shift = offset_ref[t] % LANES
        place = knot_ref[pl.ds(t, 1), :] + shift
        first = place < LANES
        lane = jnp.where(first, place, place - LANES)
        hot = (lane_row == lane.astype(F32)).astype(BF16)
        spread = jnp.concatenate([design[t, 0:8, :] * resid, design[t, 8:16, :] * resid], axis=0)
        mask = jnp.broadcast_to(first.astype(F32), spread.shape)
        here = spread * mask
        parts = split2(here) + split2(spread - here)
        outs.append(
            lax.dot_general(
                jnp.concatenate(parts, axis=0),
                hot,
                (((1,), (1,)), ((), ())),
                preferred_element_type=F32,
            )
        )
    for t, resid, out in zip(tiles, values, outs):
        slot = slot_ref[t]
        acc[slot] += design[t, 16:24, :] * resid
        row = offset_ref[t] // LANES
        knots[row] += out[0:16] + out[16:32]
        knots[row + 1] += out[32:48] + out[48:64]


def send_sums(acc, knots, piece_ref, att_ref, owners):
    for owner in range(owners):
        for param in range(PARAMS):
            piece_ref[owner * PIECE + param * CAP : owner * PIECE + param * CAP + CAP, :] = acc[
                owner * CAP : owner * CAP + CAP, param, :
            ]
    lane = iota((8, LANES), 1)
    low = iota((8, LANES), 0) < 4
    before = [jnp.zeros((8, LANES), F32)] * 3
    for row in range(ROWS + 1):
        one, two = knots[row, 0:8, :], knots[row, 8:16, :]
        now = [pltpu.roll(one, 1, 1), pltpu.roll(two, 2, 1), pltpu.roll(two, 3, 1)]
        moved = [jnp.where(lane >= k + 1, now[k], before[k]) for k in range(3)]
        both = jnp.where(low, one + moved[1], moved[0] + moved[2])
        both = both + pltpu.roll(both, 4, 0)
        for axis in range(AXES):
            att_ref[axis * ROWS_PAD + row : axis * ROWS_PAD + row + 1, :] = both[axis : axis + 1]
        before = now


def first_kernel(
    slot_ref,
    offset_ref,
    valid_ref,
    src_ref,
    att_ref,
    frac_ref,
    knot_ref,
    obs_ref,
    table_ref,
    design,
    piece_ref,
    part_ref,
    acc,
    knots,
    wts,
):
    tiles = src_ref.shape[0]
    owners = table_ref.shape[0]
    acc[...] = jnp.zeros_like(acc)
    knots[...] = jnp.zeros_like(knots)
    part_ref[...] = jnp.zeros_like(part_ref)
    for k, weight in enumerate(spline_weights(frac_ref[...])):
        wts[k] = weight
    sub = iota((8, LANES), 0)
    lane = iota((8, LANES), 1)

    def body(step, carry):
        batch = [step * UNROLL + k for k in range(UNROLL)]
        for t in batch:
            live = lane < valid_ref[t]
            three = [row_of(att_ref.at[t], axis) for axis in range(AXES)]
            axis_of = sub % 4
            mixed = jnp.where(axis_of == 0, three[0], jnp.where(axis_of == 1, three[1], three[2]))
            mixed = jnp.where(live & (axis_of < 3), mixed, 0.0)
            weights = [row_of(wts.at[k], t) for k in range(4)]
            design[t, 0:8, :] = mixed * jnp.where(sub < 4, weights[0], weights[1])
            design[t, 8:16, :] = mixed * jnp.where(sub < 4, weights[2], weights[3])
            design[t, 16:24, :] = jnp.zeros((8, LANES), F32)
            design[t, 16 : 16 + PARAMS, :] = jnp.where(live[0:PARAMS], src_ref[t], 0.0)
        values = [row_of(obs_ref, t) for t in batch]
        add_adjoint(batch, values, design, slot_ref, offset_ref, knot_ref, acc, knots)
        return carry

    lax.fori_loop(0, tiles // UNROLL, body, 0)
    send_sums(acc, knots, piece_ref, part_ref, owners)
    me = lax.axis_index("tm")
    placed = (iota((CAP, LANES), 1) == iota((CAP, LANES), 0) + me * CAP).astype(BF16)
    names = jnp.dot(
        table_ref[...].astype(F32).astype(BF16), placed, preferred_element_type=F32
    )
    for owner in range(owners):
        piece_ref[owner * PIECE + EXTRA : owner * PIECE + PIECE, :] = jnp.where(
            sub == 0, jnp.broadcast_to(names[owner : owner + 1], (8, LANES)), 0.0
        )


def owner_kernel(count, with_names, *refs):
    piece_ref, parts, rest = refs[0], refs[1 : 1 + count], refs[1 + count :]
    if with_names:
        own_ref, att_ref, back_ref, names_ref = rest
    else:
        names_in, own_in, own_ref, att_ref, back_ref = rest
    owners = piece_ref.shape[0]
    rows = owners * CAP
    sub = iota((8, LANES), 0)
    if with_names:
        names = piece_ref[0, EXTRA : EXTRA + 8, :]
        for owner in range(1, owners):
            names = names + piece_ref[owner, EXTRA : EXTRA + 8, :]
        names_ref[...] = names
    else:
        names = names_in[...]
    hot = (iota((LANES, LANES), 0).astype(F32) == jnp.broadcast_to(names[0:1], (LANES, LANES))).astype(F32)
    pick = hot[0:SB_DEV, 0:rows].astype(BF16)
    give = hot.T[0:rows, 0:SB_DEV].astype(BF16)
    pick = jnp.concatenate([pick] * 3, axis=1)
    give = jnp.concatenate([give] * 3, axis=1)
    square = jnp.zeros((SB_DEV, LANES), F32)
    if not with_names:
        sums = piece_ref[0, EXTRA : EXTRA + 8, :]
        for owner in range(1, owners):
            sums = sums + piece_ref[owner, EXTRA : EXTRA + 8, :]
        sigma = sums[1:2, 0:1] / sums[1:2, 1:2]
        across = jnp.zeros((SB_DEV, LANES), F32)
    for param in range(PARAMS):
        got = piece_ref[:, param * CAP : param * CAP + CAP, :].reshape(rows, LANES)
        mine = jnp.dot(pick, jnp.concatenate(split3(got), axis=0), preferred_element_type=F32)
        own_ref[param] = mine
        back = jnp.dot(give, jnp.concatenate(split3(mine), axis=0), preferred_element_type=F32)
        back_ref[:, param * CAP : param * CAP + CAP, :] = back.reshape(owners, CAP, LANES)
        if with_names:
            square = square + mine * mine
        else:
            before = own_in[param]
            rest_ = mine - sigma * before
            square = square + rest_ * rest_
            across = across + rest_ * before
    level = [part[...] for part in parts]
    while len(level) > 1:
        level = [level[k] + level[k + 1] for k in range(0, len(level), 2)]
    att_ref[...] = level[0]
    extra = jnp.zeros((8, LANES), F32)
    for axis in range(AXES):
        at = axis * ROWS_PAD
        extra = jnp.where(sub == axis, level[0][at : at + 1], extra)
        extra = jnp.where(sub == AXES + axis, level[0][at + ROWS : at + ROWS + 1], extra)
    lane = iota((8, LANES), 1)
    numbers = jnp.where(lane == 0, total(square), 0.0)
    if not with_names:
        numbers = jnp.where(lane == 1, total(across), numbers)
        numbers = jnp.where(lane == 2, sigma, numbers)
        numbers = jnp.where(lane == 3, sums[1:2, 0:1], numbers)
        numbers = jnp.where(lane == 4, sums[1:2, 1:2], numbers)
    extra = jnp.where(sub == 2 * AXES, numbers, extra)
    for owner in range(owners):
        back_ref[owner, EXTRA : EXTRA + 8, :] = extra


def load_vector(got_ref, part_ref, slots, table, true_ref):
    owners = got_ref.shape[0] // PIECE
    me = lax.axis_index("tm")
    slots[...] = jnp.zeros_like(slots)
    for owner in range(owners):
        for param in range(PARAMS):
            slots[owner * CAP : owner * CAP + CAP, param, :] = got_ref[
                owner * PIECE + param * CAP : owner * PIECE + param * CAP + CAP, :
            ]
    left = got_ref[pl.ds(jnp.maximum(me - 1, 0) * PIECE + EXTRA, 8), :]
    right = got_ref[pl.ds(jnp.minimum(me + 1, owners - 1) * PIECE + EXTRA, 8), :]
    left = jnp.where(me > 0, left, 0.0)
    right = jnp.where(me < owners - 1, right, 0.0)
    has_right = jnp.where(me < owners - 1, 1.0, 0.0)
    sub = iota((8, LANES), 0)
    lane = iota((8, LANES), 1)
    low = sub < 4
    axis_of = sub % 4
    for axis in range(AXES):
        at = axis * ROWS_PAD
        true_ref[axis] = part_ref[at : at + ROWS, :]
        true_ref[axis, 0:1, :] = part_ref[at : at + 1, :] + left[AXES + axis : AXES + axis + 1]

    def mixed(row):
        if row < ROWS:
            three = [true_ref[axis, row : row + 1, :] for axis in range(AXES)]
        else:
            three = [
                right[axis : axis + 1] + has_right * part_ref[axis * ROWS_PAD + ROWS : axis * ROWS_PAD + ROWS + 1, :]
                for axis in range(AXES)
            ]
        three = [jnp.broadcast_to(v, (8, LANES)) for v in three]
        out = jnp.where(axis_of == 0, three[0], jnp.where(axis_of == 1, three[1], three[2]))
        return jnp.where(axis_of < 3, out, 0.0)

    def rolled(value):
        return [pltpu.roll(value, LANES - k, 1) for k in (1, 2, 3)]

    now = mixed(0)
    now_rolled = rolled(now)
    for row in range(ROWS + 1):
        after = mixed(row + 1) if row < ROWS else jnp.zeros((8, LANES), F32)
        after_rolled = rolled(after)
        moved = [jnp.where(lane < LANES - 1 - k, now_rolled[k], after_rolled[k]) for k in range(3)]
        table[row, 0:8, :] = jnp.where(low, now, moved[0])
        table[row, 8:16, :] = jnp.where(low, moved[1], moved[2])
        now, now_rolled = after, after_rolled


def forward(tiles, design, slot_ref, offset_ref, knot_ref, slots, table):
    values = []
    for t in tiles:
        shift = offset_ref[t] % LANES
        row = offset_ref[t] // LANES
        place = row_of(knot_ref, t) + shift
        first = place < LANES
        lane = jnp.where(first, place, place - LANES)
        summed = design[t, 16:24, :] * slots[slot_ref[t]]
        for half in (0, 8):
            here = jnp.take_along_axis(table[row, half : half + 8, :], lane, axis=1)
            there = jnp.take_along_axis(table[row + 1, half : half + 8, :], lane, axis=1)
            summed = summed + design[t, half : half + 8, :] * jnp.where(first, here, there)
        summed = summed + pltpu.roll(summed, 4, 0)
        summed = summed + pltpu.roll(summed, 2, 0)
        values.append(summed + pltpu.roll(summed, 1, 0))
    return values


def middle_kernel(
    copies,
    slot_ref,
    offset_ref,
    got_ref,
    part_ref,
    design,
    knot_ref,
    piece_ref,
    sum_ref,
    true_ref,
    y_ref,
    acc,
    knots,
    slots,
    table,
):
    tiles = design.shape[0]
    owners = got_ref.shape[0] // PIECE
    acc[...] = jnp.zeros_like(acc)
    knots[...] = jnp.zeros_like(knots)
    sum_ref[...] = jnp.zeros_like(sum_ref)
    load_vector(got_ref, part_ref, slots, table, true_ref)

    def body(step, square):
        batch = [step * UNROLL + k for k in range(UNROLL)]
        values = forward(batch, design, slot_ref, offset_ref, knot_ref, slots, table)
        for t, value in zip(batch, values):
            y_ref[pl.ds(t, 1), :] = value[0:1]
            square = square + value * value
        add_adjoint(batch, values, design, slot_ref, offset_ref, knot_ref, acc, knots)
        return square

    square = lax.fori_loop(0, tiles // UNROLL, body, jnp.zeros((8, LANES), F32))
    send_sums(acc, knots, piece_ref, sum_ref, owners)
    norm_att = jnp.zeros((ROWS, LANES), F32)
    for axis in range(AXES):
        norm_att = norm_att + true_ref[axis] * true_ref[axis]
    me = lax.axis_index("tm")
    sent = got_ref[pl.ds(me * PIECE + EXTRA, 8), :]
    norm = sent[2 * AXES : 2 * AXES + 1, 0:1] + total(norm_att) / copies
    lane = iota((8, LANES), 1)
    numbers = jnp.where(lane == 0, total(square[0:1]), jnp.where(lane == 1, norm, 0.0))
    numbers = jnp.where(iota((8, LANES), 0) == 1, numbers, 0.0)
    for owner in range(owners):
        piece_ref[owner * PIECE + EXTRA : owner * PIECE + PIECE, :] = numbers


def last_kernel(
    copies,
    slot_ref,
    offset_ref,
    got_ref,
    part_ref,
    design,
    knot_ref,
    y_ref,
    numbers_ref,
    before_ref,
    true_ref,
    out_ref,
    slots,
    table,
):
    tiles = design.shape[0]
    owners = got_ref.shape[0] // PIECE
    load_vector(got_ref, part_ref, slots, table, true_ref)
    me = lax.axis_index("tm")
    sent = got_ref[pl.ds(me * PIECE + EXTRA, 8), :][2 * AXES : 2 * AXES + 1]
    group = got_ref[EXTRA : EXTRA + 8, :]
    for owner in range(1, owners):
        group = group + got_ref[owner * PIECE + EXTRA : owner * PIECE + EXTRA + 8, :]
    group = group[2 * AXES : 2 * AXES + 1]
    sigma, s_group, n_group = sent[:, 2:3], sent[:, 3:4], sent[:, 4:5]
    square_att = jnp.zeros((ROWS, LANES), F32)
    across_att = jnp.zeros((ROWS, LANES), F32)
    for axis in range(AXES):
        rest = true_ref[axis] - sigma * before_ref[axis]
        square_att = square_att + rest * rest
        across_att = across_att + rest * before_ref[axis]
    square_att = total(square_att) / copies
    across_att = total(across_att) / copies
    d_group = group[:, 0:1] + square_att * owners
    tau = sigma + d_group / (s_group + n_group)
    tau_full = jnp.broadcast_to(tau, (8, LANES))

    def body(step, carry):
        square, across = carry
        batch = [step * UNROLL + k for k in range(UNROLL)]
        values = forward(batch, design, slot_ref, offset_ref, knot_ref, slots, table)
        for t, value in zip(batch, values):
            before = row_of(y_ref, t)
            rest = value - tau_full * before
            square = square + rest * rest
            across = across + rest * before
        return square, across

    zero = jnp.zeros((8, LANES), F32)
    square, across = lax.fori_loop(0, tiles // UNROLL, body, (zero, zero))
    own = numbers_ref[...][EXTRA + 1 : EXTRA + 2]
    numbers = [
        own[:, 1:2],
        own[:, 0:1],
        sent[:, 0:1] + square_att,
        sent[:, 1:2] + across_att,
        sigma,
        total(square[0:1]),
        total(across[0:1]),
        tau,
    ]
    lane = iota((1, LANES), 1)
    out = jnp.zeros((1, LANES), F32)
    for k, number in enumerate(numbers):
        out = jnp.where(lane == k, number, out)
    out_ref[...] = jnp.broadcast_to(out[None], out_ref.shape)


def final_kernel(got_ref, z_src, w_src, z_att, w_att, src_out, att_out):
    devices = got_ref.shape[0]
    got = got_ref[...].reshape(devices, LANES)

    def column(k):
        return got[:, k : k + 1]

    def summed(value):
        return jnp.sum(value, axis=0, keepdims=True)

    n_of, s_of = column(0), column(1)
    n, s = summed(n_of), summed(s_of)
    sigma = s / n
    alpha = n / (s + n)
    off = column(4) - sigma
    d = summed(column(2) + 2.0 * off * column(3) + off * off * n_of)
    gamma = alpha * d / n
    tau = sigma + gamma
    off = column(7) - tau
    e = summed(column(5) + 2.0 * off * column(6) + off * off * s_of)
    second = d / (e + damping * (d + gamma * gamma * n))
    c_z = alpha * (1.0 + second * tau)
    c_w = alpha * second
    for param in range(PARAMS):
        src_out[:, param, :] = c_z * z_src[param] - c_w * w_src[param]
    for axis in range(AXES):
        value = c_z * z_att[axis] - c_w * w_att[axis]
        for row in range(ROWS):
            att_out[axis : axis + 1, row * LANES : (row + 1) * LANES] = value[row : row + 1]


VMEM = pl.BlockSpec(memory_space=pltpu.VMEM)
SMEM = pl.BlockSpec(memory_space=pltpu.SMEM)
PARAMETERS = pltpu.CompilerParams(vmem_limit_bytes=24 * 1024 * 1024)


def f32(*shape):
    return jax.ShapeDtypeStruct(shape, F32)


def call(kernel, out_shape, in_specs, scratch=(), name=None):
    return pl.pallas_call(
        kernel,
        out_shape=out_shape,
        in_specs=in_specs,
        out_specs=jax.tree.map(lambda _: VMEM, out_shape),
        scratch_shapes=list(scratch),
        compiler_params=PARAMETERS,
        name=name,
    )


def shards(
    src_design,
    att_design,
    obs_frac,
    obs_knot,
    observed,
    tile_slot,
    tile_offset,
    tile_valid,
    slot_block,
):
    tiles = src_design.shape[0]
    owners = lax.axis_size("tm")
    copies = lax.axis_size("src")
    devices = owners * copies
    slot_count = owners * CAP
    acc = pltpu.VMEM((slot_count, 8, LANES), F32)
    knots = pltpu.VMEM((ROWS + 1, 16, LANES), F32)
    piece = f32(owners * PIECE, LANES)
    part = f32(AXES * ROWS_PAD, LANES)
    true = f32(AXES, ROWS, LANES)

    def exchange(pieces):
        return lax.all_to_all(pieces.reshape(owners, PIECE, LANES), "tm", 0, 0, tiled=True)

    def src_parts(own):
        return [own] + [
            lax.ppermute(own, "src", [(i, i ^ k) for i in range(copies)]) for k in range(1, copies)
        ]

    design, pieces, own = call(
        first_kernel,
        (f32(tiles, 24, LANES), piece, part),
        [SMEM] * 3 + [VMEM] * 6,
        [acc, knots, pltpu.VMEM((4, tiles, LANES), F32)],
        "first",
    )(tile_slot, tile_offset, tile_valid, src_design, att_design, obs_frac, obs_knot, observed, slot_block)
    got, parts = exchange(pieces), src_parts(own)
    z_src, z_part, back, names = call(
        functools.partial(owner_kernel, copies, True),
        (f32(PARAMS, SB_DEV, LANES), part, f32(owners, PIECE, LANES), f32(8, LANES)),
        [VMEM] * (1 + copies),
        name="owner_first",
    )(got, *parts)
    got = exchange(back).reshape(owners * PIECE, LANES)
    pieces, own, z_att, y = call(
        functools.partial(middle_kernel, copies),
        (piece, part, true, f32(tiles, LANES)),
        [SMEM] * 2 + [VMEM] * 4,
        [acc, knots, acc, knots],
        "middle",
    )(tile_slot, tile_offset, got, z_part, design, obs_knot)
    numbers = pieces
    got, parts = exchange(pieces), src_parts(own)
    w_src, w_part, back = call(
        functools.partial(owner_kernel, copies, False),
        (f32(PARAMS, SB_DEV, LANES), part, f32(owners, PIECE, LANES)),
        [VMEM] * (3 + copies),
        name="owner_second",
    )(got, *parts, names, z_src)
    got = exchange(back).reshape(owners * PIECE, LANES)
    w_att, row = call(
        functools.partial(last_kernel, copies),
        (true, f32(devices, 1, LANES)),
        [SMEM] * 2 + [VMEM] * 7,
        [acc, knots],
        "last",
    )(tile_slot, tile_offset, got, w_part, design, obs_knot, y, numbers, z_att)
    row = lax.all_to_all(row, ("src", "tm"), 0, 0, tiled=True)
    return call(
        final_kernel,
        (f32(SB_DEV, PARAMS, LANES), f32(AXES, KN)),
        [VMEM] * 5,
        name="final",
    )(row, z_src, w_src, z_att, w_att)


def solution(mesh):
    placed = (
        P(("src", "tm"), None, None),
        P(("src", "tm"), None, None),
        P(("src", "tm"), None),
        P(("src", "tm"), None),
        P(("src", "tm"), None),
        P(("src", "tm")),
        P(("src", "tm")),
        P(("src", "tm")),
        P(("src", "tm"), None),
    )
    return jax.shard_map(
        shards,
        mesh=mesh,
        in_specs=placed,
        out_specs=(P(("src", "tm"), None, None), P(None, "tm")),
        check_vma=False,
    )
```

```python
import functools

import jax
import jax.numpy as jnp
from jax import lax
from jax.experimental import pallas as pl
from jax.experimental.pallas import tpu as pltpu
from jax.sharding import PartitionSpec as P

KN = 4096
HW = 128
SB_DEV = 32
damping = 1.0

LANES = 128
ROWS = KN // LANES
ROWS_PAD = (ROWS + 8) // 8 * 8
AXES = 3
PARAMS = 5
CAP = 8
EXTRA = PARAMS * CAP
PIECE = EXTRA + 8
UNROLL = 32
F32 = jnp.float32
BF16 = jnp.bfloat16


def iota(shape, dim):
    return lax.broadcasted_iota(jnp.int32, shape, dim)


def spline_weights(fraction):
    remain = 1.0 - fraction
    square = fraction * fraction
    cubed = square * fraction
    return (
        remain * remain * remain / 6.0,
        (3.0 * cubed - 6.0 * square + 4.0) / 6.0,
        (-3.0 * cubed + 3.0 * square + 3.0 * fraction + 1.0) / 6.0,
        cubed / 6.0,
    )


def split2(value):
    high = value.astype(BF16)
    return high, (value - high.astype(F32)).astype(BF16)


def split3(value):
    high, rest = value.astype(BF16), None
    rest = value - high.astype(F32)
    middle = rest.astype(BF16)
    return high, middle, (rest - middle.astype(F32)).astype(BF16)


def total(value):
    return jnp.sum(jnp.sum(value, axis=0, keepdims=True), axis=1, keepdims=True)


def row_of(ref, row):
    return jnp.broadcast_to(ref[pl.ds(row, 1), :], (8, LANES))


def add_adjoint(tiles, values, design, slot_ref, offset_ref, knot_ref, acc, knots):
    lane_row = iota((LANES, LANES), 0).astype(F32).astype(BF16)
    yes, no = jnp.ones((), BF16), jnp.zeros((), BF16)
    outs = []
    for t, resid in zip(tiles, values):
        shift = offset_ref[t] % LANES
        place = knot_ref[pl.ds(t, 1), :] + shift
        first = place < LANES
        lane = jnp.where(first, place, place - LANES)
        hot = jnp.where(lane_row == lane.astype(F32).astype(BF16), yes, no)
        spread = jnp.concatenate([design[t, 0:8, :] * resid, design[t, 8:16, :] * resid], axis=0)
        mask = jnp.broadcast_to(first.astype(F32), spread.shape)
        here = spread * mask
        parts = split2(here) + split2(spread - here)
        outs.append(
            lax.dot_general(
                jnp.concatenate(parts, axis=0),
                hot,
                (((1,), (1,)), ((), ())),
                preferred_element_type=F32,
            )
        )
    for t, resid, out in zip(tiles, values, outs):
        slot = slot_ref[t]
        acc[slot] += design[t, 16:24, :] * resid
        row = offset_ref[t] // LANES
        knots[row] += out[0:16] + out[16:32]
        knots[row + 1] += out[32:48] + out[48:64]


def send_sums(acc, knots, piece_ref, att_ref, owners):
    for owner in range(owners):
        for param in range(PARAMS):
            piece_ref[owner * PIECE + param * CAP : owner * PIECE + param * CAP + CAP, :] = acc[
                owner * CAP : owner * CAP + CAP, param, :
            ]
    lane = iota((8, LANES), 1)
    low = iota((8, LANES), 0) < 4
    before = [jnp.zeros((8, LANES), F32)] * 3
    for row in range(ROWS + 1):
        one, two = knots[row, 0:8, :], knots[row, 8:16, :]
        now = [pltpu.roll(one, 1, 1), pltpu.roll(two, 2, 1), pltpu.roll(two, 3, 1)]
        moved = [jnp.where(lane >= k + 1, now[k], before[k]) for k in range(3)]
        both = jnp.where(low, one + moved[1], moved[0] + moved[2])
        both = both + pltpu.roll(both, 4, 0)
        for axis in range(AXES):
            att_ref[axis * ROWS_PAD + row : axis * ROWS_PAD + row + 1, :] = both[axis : axis + 1]
        before = now


def first_kernel(
    slot_hbm,
    offset_hbm,
    valid_hbm,
    src_hbm,
    att_hbm,
    frac_hbm,
    knot_hbm,
    obs_hbm,
    table_hbm,
    design,
    piece_ref,
    part_ref,
    acc,
    knots,
    wts,
    slot_ref,
    offset_ref,
    valid_ref,
    src_ref,
    att_ref,
    frac_ref,
    knot_ref,
    obs_ref,
    table_ref,
    sems,
):
    pairs = (
        (frac_hbm, frac_ref),
        (offset_hbm, offset_ref),
        (valid_hbm, valid_ref),
        (slot_hbm, slot_ref),
        (knot_hbm, knot_ref),
        (obs_hbm, obs_ref),
        (att_hbm, att_ref),
        (src_hbm, src_ref),
        (table_hbm, table_ref),
    )
    copies = [pltpu.make_async_copy(a, b, sems.at[k]) for k, (a, b) in enumerate(pairs)]
    for copy in copies:
        copy.start()
    tiles = knot_ref.shape[0]
    owners = table_ref.shape[0]
    acc[...] = jnp.zeros_like(acc)
    knots[...] = jnp.zeros_like(knots)
    part_ref[...] = jnp.zeros_like(part_ref)
    for copy in copies:
        copy.wait()
    for k, weight in enumerate(spline_weights(frac_ref[...])):
        wts[k] = weight
    sub = iota((8, LANES), 0)
    lane = iota((8, LANES), 1)

    def body(step, carry):
        batch = [step * UNROLL + k for k in range(UNROLL)]
        for t in batch:
            live = lane < valid_ref[t]
            three = [row_of(att_ref, axis * tiles + t) for axis in range(AXES)]
            axis_of = sub % 4
            mixed = jnp.where(axis_of == 0, three[0], jnp.where(axis_of == 1, three[1], three[2]))
            mixed = jnp.where(live & (axis_of < 3), mixed, 0.0)
            weights = [row_of(wts.at[k], t) for k in range(4)]
            design[t, 0:8, :] = mixed * jnp.where(sub < 4, weights[0], weights[1])
            design[t, 8:16, :] = mixed * jnp.where(sub < 4, weights[2], weights[3])
            design[t, 16:24, :] = jnp.zeros((8, LANES), F32)
            design[t, 16 : 16 + PARAMS, :] = jnp.where(
                live[0:PARAMS], src_ref[pl.ds(t, PARAMS, stride=tiles), :], 0.0
            )
        values = [row_of(obs_ref, t) for t in batch]
        add_adjoint(batch, values, design, slot_ref, offset_ref, knot_ref, acc, knots)
        return carry

    lax.fori_loop(0, tiles // UNROLL, body, 0)
    send_sums(acc, knots, piece_ref, part_ref, owners)
    me = lax.axis_index("tm")
    placed = (iota((CAP, LANES), 1) == iota((CAP, LANES), 0) + me * CAP).astype(BF16)
    names = jnp.dot(
        table_ref[...].astype(F32).astype(BF16), placed, preferred_element_type=F32
    )
    for owner in range(owners):
        piece_ref[owner * PIECE + EXTRA : owner * PIECE + PIECE, :] = jnp.where(
            sub == 0, jnp.broadcast_to(names[owner : owner + 1], (8, LANES)), 0.0
        )


def owner_kernel(count, with_names, *refs):
    piece_ref, parts, rest = refs[0], refs[1 : 1 + count], refs[1 + count :]
    if with_names:
        own_ref, att_ref, back_ref, names_ref = rest
    else:
        names_in, own_in, own_ref, att_ref, back_ref = rest
    owners = piece_ref.shape[0]
    rows = owners * CAP
    sub = iota((8, LANES), 0)
    if with_names:
        names = piece_ref[0, EXTRA : EXTRA + 8, :]
        for owner in range(1, owners):
            names = names + piece_ref[owner, EXTRA : EXTRA + 8, :]
        names_ref[...] = names
    else:
        names = names_in[...]
    hot = (iota((LANES, LANES), 0).astype(F32) == jnp.broadcast_to(names[0:1], (LANES, LANES))).astype(F32)
    pick = hot[0:SB_DEV, 0:rows].astype(BF16)
    give = hot.T[0:rows, 0:SB_DEV].astype(BF16)
    pick = jnp.concatenate([pick] * 3, axis=1)
    give = jnp.concatenate([give] * 3, axis=1)
    square = jnp.zeros((SB_DEV, LANES), F32)
    if not with_names:
        sums = piece_ref[0, EXTRA : EXTRA + 8, :]
        for owner in range(1, owners):
            sums = sums + piece_ref[owner, EXTRA : EXTRA + 8, :]
        sigma = sums[1:2, 0:1] / sums[1:2, 1:2]
        across = jnp.zeros((SB_DEV, LANES), F32)
    for param in range(PARAMS):
        got = piece_ref[:, param * CAP : param * CAP + CAP, :].reshape(rows, LANES)
        mine = jnp.dot(pick, jnp.concatenate(split3(got), axis=0), preferred_element_type=F32)
        own_ref[param] = mine
        back = jnp.dot(give, jnp.concatenate(split3(mine), axis=0), preferred_element_type=F32)
        back_ref[:, param * CAP : param * CAP + CAP, :] = back.reshape(owners, CAP, LANES)
        if with_names:
            square = square + mine * mine
        else:
            before = own_in[param]
            rest_ = mine - sigma * before
            square = square + rest_ * rest_
            across = across + rest_ * before
    level = [part[...] for part in parts]
    while len(level) > 1:
        level = [level[k] + level[k + 1] for k in range(0, len(level), 2)]
    att_ref[...] = level[0]
    extra = jnp.zeros((8, LANES), F32)
    for axis in range(AXES):
        at = axis * ROWS_PAD
        extra = jnp.where(sub == axis, level[0][at : at + 1], extra)
        extra = jnp.where(sub == AXES + axis, level[0][at + ROWS : at + ROWS + 1], extra)
    lane = iota((8, LANES), 1)
    numbers = jnp.where(lane == 0, total(square), 0.0)
    if not with_names:
        numbers = jnp.where(lane == 1, total(across), numbers)
        numbers = jnp.where(lane == 2, sigma, numbers)
        numbers = jnp.where(lane == 3, sums[1:2, 0:1], numbers)
        numbers = jnp.where(lane == 4, sums[1:2, 1:2], numbers)
    extra = jnp.where(sub == 2 * AXES, numbers, extra)
    for owner in range(owners):
        back_ref[owner, EXTRA : EXTRA + 8, :] = extra


def load_vector(got_ref, part_ref, slots, table, true_ref):
    owners = got_ref.shape[0] // PIECE
    me = lax.axis_index("tm")
    slots[...] = jnp.zeros_like(slots)
    for owner in range(owners):
        for param in range(PARAMS):
            slots[owner * CAP : owner * CAP + CAP, param, :] = got_ref[
                owner * PIECE + param * CAP : owner * PIECE + param * CAP + CAP, :
            ]
    left = got_ref[pl.ds(jnp.maximum(me - 1, 0) * PIECE + EXTRA, 8), :]
    right = got_ref[pl.ds(jnp.minimum(me + 1, owners - 1) * PIECE + EXTRA, 8), :]
    left = jnp.where(me > 0, left, 0.0)
    right = jnp.where(me < owners - 1, right, 0.0)
    has_right = jnp.where(me < owners - 1, 1.0, 0.0)
    sub = iota((8, LANES), 0)
    lane = iota((8, LANES), 1)
    low = sub < 4
    axis_of = sub % 4
    for axis in range(AXES):
        at = axis * ROWS_PAD
        true_ref[axis] = part_ref[at : at + ROWS, :]
        true_ref[axis, 0:1, :] = part_ref[at : at + 1, :] + left[AXES + axis : AXES + axis + 1]

    def mixed(row):
        if row < ROWS:
            three = [true_ref[axis, row : row + 1, :] for axis in range(AXES)]
        else:
            three = [
                right[axis : axis + 1] + has_right * part_ref[axis * ROWS_PAD + ROWS : axis * ROWS_PAD + ROWS + 1, :]
                for axis in range(AXES)
            ]
        three = [jnp.broadcast_to(v, (8, LANES)) for v in three]
        out = jnp.where(axis_of == 0, three[0], jnp.where(axis_of == 1, three[1], three[2]))
        return jnp.where(axis_of < 3, out, 0.0)

    def rolled(value):
        return [pltpu.roll(value, LANES - k, 1) for k in (1, 2, 3)]

    now = mixed(0)
    now_rolled = rolled(now)
    for row in range(ROWS + 1):
        after = mixed(row + 1) if row < ROWS else jnp.zeros((8, LANES), F32)
        after_rolled = rolled(after)
        moved = [jnp.where(lane < LANES - 1 - k, now_rolled[k], after_rolled[k]) for k in range(3)]
        table[row, 0:8, :] = jnp.where(low, now, moved[0])
        table[row, 8:16, :] = jnp.where(low, moved[1], moved[2])
        now, now_rolled = after, after_rolled


def forward(tiles, design, slot_ref, offset_ref, knot_ref, slots, table):
    values = []
    for t in tiles:
        shift = offset_ref[t] % LANES
        row = offset_ref[t] // LANES
        place = row_of(knot_ref, t) + shift
        first = place < LANES
        lane = jnp.where(first, place, place - LANES)
        summed = design[t, 16:24, :] * slots[slot_ref[t]]
        for half in (0, 8):
            here = jnp.take_along_axis(table[row, half : half + 8, :], lane, axis=1)
            there = jnp.take_along_axis(table[row + 1, half : half + 8, :], lane, axis=1)
            summed = summed + design[t, half : half + 8, :] * jnp.where(first, here, there)
        summed = summed + pltpu.roll(summed, 4, 0)
        summed = summed + pltpu.roll(summed, 2, 0)
        values.append(summed + pltpu.roll(summed, 1, 0))
    return values


def middle_kernel(
    copies,
    slot_ref,
    offset_ref,
    got_ref,
    part_ref,
    design,
    knot_ref,
    piece_ref,
    sum_ref,
    true_ref,
    y_ref,
    acc,
    knots,
    slots,
    table,
):
    tiles = design.shape[0]
    owners = got_ref.shape[0] // PIECE
    acc[...] = jnp.zeros_like(acc)
    knots[...] = jnp.zeros_like(knots)
    sum_ref[...] = jnp.zeros_like(sum_ref)
    load_vector(got_ref, part_ref, slots, table, true_ref)

    def body(step, square):
        batch = [step * UNROLL + k for k in range(UNROLL)]
        values = forward(batch, design, slot_ref, offset_ref, knot_ref, slots, table)
        for t, value in zip(batch, values):
            y_ref[pl.ds(t, 1), :] = value[0:1]
            square = square + value * value
        add_adjoint(batch, values, design, slot_ref, offset_ref, knot_ref, acc, knots)
        return square

    square = lax.fori_loop(0, tiles // UNROLL, body, jnp.zeros((8, LANES), F32))
    send_sums(acc, knots, piece_ref, sum_ref, owners)
    norm_att = jnp.zeros((ROWS, LANES), F32)
    for axis in range(AXES):
        norm_att = norm_att + true_ref[axis] * true_ref[axis]
    me = lax.axis_index("tm")
    sent = got_ref[pl.ds(me * PIECE + EXTRA, 8), :]
    norm = sent[2 * AXES : 2 * AXES + 1, 0:1] + total(norm_att) / copies
    lane = iota((8, LANES), 1)
    numbers = jnp.where(lane == 0, total(square[0:1]), jnp.where(lane == 1, norm, 0.0))
    numbers = jnp.where(iota((8, LANES), 0) == 1, numbers, 0.0)
    for owner in range(owners):
        piece_ref[owner * PIECE + EXTRA : owner * PIECE + PIECE, :] = numbers


def last_kernel(
    copies,
    slot_ref,
    offset_ref,
    got_ref,
    part_ref,
    design,
    knot_ref,
    y_ref,
    numbers_ref,
    before_ref,
    true_ref,
    out_ref,
    slots,
    table,
):
    tiles = design.shape[0]
    owners = got_ref.shape[0] // PIECE
    load_vector(got_ref, part_ref, slots, table, true_ref)
    me = lax.axis_index("tm")
    sent = got_ref[pl.ds(me * PIECE + EXTRA, 8), :][2 * AXES : 2 * AXES + 1]
    group = got_ref[EXTRA : EXTRA + 8, :]
    for owner in range(1, owners):
        group = group + got_ref[owner * PIECE + EXTRA : owner * PIECE + EXTRA + 8, :]
    group = group[2 * AXES : 2 * AXES + 1]
    sigma, s_group, n_group = sent[:, 2:3], sent[:, 3:4], sent[:, 4:5]
    square_att = jnp.zeros((ROWS, LANES), F32)
    across_att = jnp.zeros((ROWS, LANES), F32)
    for axis in range(AXES):
        rest = true_ref[axis] - sigma * before_ref[axis]
        square_att = square_att + rest * rest
        across_att = across_att + rest * before_ref[axis]
    square_att = total(square_att) / copies
    across_att = total(across_att) / copies
    d_group = group[:, 0:1] + square_att * owners
    tau = sigma + d_group / (s_group + n_group)
    tau_full = jnp.broadcast_to(tau, (8, LANES))

    def body(step, carry):
        square, across = carry
        batch = [step * UNROLL + k for k in range(UNROLL)]
        values = forward(batch, design, slot_ref, offset_ref, knot_ref, slots, table)
        for t, value in zip(batch, values):
            before = row_of(y_ref, t)
            rest = value - tau_full * before
            square = square + rest * rest
            across = across + rest * before
        return square, across

    zero = jnp.zeros((8, LANES), F32)
    square, across = lax.fori_loop(0, tiles // UNROLL, body, (zero, zero))
    own = numbers_ref[...][EXTRA + 1 : EXTRA + 2]
    numbers = [
        own[:, 1:2],
        own[:, 0:1],
        sent[:, 0:1] + square_att,
        sent[:, 1:2] + across_att,
        sigma,
        total(square[0:1]),
        total(across[0:1]),
        tau,
    ]
    lane = iota((1, LANES), 1)
    out = jnp.zeros((1, LANES), F32)
    for k, number in enumerate(numbers):
        out = jnp.where(lane == k, number, out)
    out_ref[...] = jnp.broadcast_to(out[None], out_ref.shape)


def final_kernel(got_ref, z_src, w_src, z_att, w_att, src_out, att_out):
    devices = got_ref.shape[0]
    got = got_ref[...].reshape(devices, LANES)

    def column(k):
        return got[:, k : k + 1]

    def summed(value):
        return jnp.sum(value, axis=0, keepdims=True)

    n_of, s_of = column(0), column(1)
    n, s = summed(n_of), summed(s_of)
    sigma = s / n
    alpha = n / (s + n)
    off = column(4) - sigma
    d = summed(column(2) + 2.0 * off * column(3) + off * off * n_of)
    gamma = alpha * d / n
    tau = sigma + gamma
    off = column(7) - tau
    e = summed(column(5) + 2.0 * off * column(6) + off * off * s_of)
    second = d / (e + damping * (d + gamma * gamma * n))
    c_z = alpha * (1.0 + second * tau)
    c_w = alpha * second
    for param in range(PARAMS):
        src_out[param] = c_z * z_src[param] - c_w * w_src[param]
    for axis in range(AXES):
        value = c_z * z_att[axis] - c_w * w_att[axis]
        for row in range(ROWS):
            att_out[axis : axis + 1, row * LANES : (row + 1) * LANES] = value[row : row + 1]


VMEM = pl.BlockSpec(memory_space=pltpu.VMEM)
SMEM = pl.BlockSpec(memory_space=pltpu.SMEM)
HBM = pl.BlockSpec(memory_space=pltpu.HBM)
PARAMETERS = pltpu.CompilerParams(vmem_limit_bytes=24 * 1024 * 1024)


def f32(*shape):
    return jax.ShapeDtypeStruct(shape, F32)


def call(kernel, out_shape, in_specs, scratch=(), name=None):
    return pl.pallas_call(
        kernel,
        out_shape=out_shape,
        in_specs=in_specs,
        out_specs=jax.tree.map(lambda _: VMEM, out_shape),
        scratch_shapes=list(scratch),
        compiler_params=PARAMETERS,
        name=name,
    )


def shards(
    src_design,
    att_design,
    obs_frac,
    obs_knot,
    observed,
    tile_slot,
    tile_offset,
    tile_valid,
    slot_block,
):
    tiles = src_design.shape[0]
    owners = lax.axis_size("tm")
    copies = lax.axis_size("src")
    devices = owners * copies
    slot_count = owners * CAP
    acc = pltpu.VMEM((slot_count, 8, LANES), F32)
    knots = pltpu.VMEM((ROWS + 1, 16, LANES), F32)
    piece = f32(owners * PIECE, LANES)
    part = f32(AXES * ROWS_PAD, LANES)
    true = f32(AXES, ROWS, LANES)

    def exchange(pieces):
        return lax.all_to_all(pieces.reshape(owners, PIECE, LANES), "tm", 0, 0, tiled=True)

    def src_parts(own):
        return [own] + [
            lax.ppermute(own, "src", [(i, i ^ k) for i in range(copies)]) for k in range(1, copies)
        ]

    src_rows = jnp.transpose(src_design, (1, 0, 2)).reshape(PARAMS * tiles, LANES)
    att_rows = jnp.transpose(att_design, (1, 0, 2)).reshape(AXES * tiles, LANES)
    inputs = (tile_slot, tile_offset, tile_valid, src_rows, att_rows, obs_frac, obs_knot, observed, slot_block)
    design, pieces, own = call(
        first_kernel,
        (f32(tiles, 24, LANES), piece, part),
        [HBM] * len(inputs),
        [acc, knots, pltpu.VMEM((4, tiles, LANES), F32)]
        + [pltpu.SMEM((tiles,), jnp.int32)] * 3
        + [pltpu.VMEM(value.shape, value.dtype) for value in inputs[3:]]
        + [pltpu.SemaphoreType.DMA((len(inputs),))],
        "first",
    )(*[pltpu.with_memory_space_constraint(value, pltpu.HBM) for value in inputs])
    got, parts = exchange(pieces), src_parts(own)
    z_src, z_part, back, names = call(
        functools.partial(owner_kernel, copies, True),
        (f32(PARAMS, SB_DEV, LANES), part, f32(owners, PIECE, LANES), f32(8, LANES)),
        [VMEM] * (1 + copies),
        name="owner_first",
    )(got, *parts)
    got = exchange(back).reshape(owners * PIECE, LANES)
    pieces, own, z_att, y = call(
        functools.partial(middle_kernel, copies),
        (piece, part, true, f32(tiles, LANES)),
        [SMEM] * 2 + [VMEM] * 4,
        [acc, knots, acc, knots],
        "middle",
    )(tile_slot, tile_offset, got, z_part, design, obs_knot)
    numbers = pieces
    got, parts = exchange(pieces), src_parts(own)
    w_src, w_part, back = call(
        functools.partial(owner_kernel, copies, False),
        (f32(PARAMS, SB_DEV, LANES), part, f32(owners, PIECE, LANES)),
        [VMEM] * (3 + copies),
        name="owner_second",
    )(got, *parts, names, z_src)
    got = exchange(back).reshape(owners * PIECE, LANES)
    w_att, row = call(
        functools.partial(last_kernel, copies),
        (true, f32(devices, 1, LANES)),
        [SMEM] * 2 + [VMEM] * 7,
        [acc, knots],
        "last",
    )(tile_slot, tile_offset, got, w_part, design, obs_knot, y, numbers, z_att)
    row = lax.all_to_all(row, ("src", "tm"), 0, 0, tiled=True)
    src, att = call(
        final_kernel,
        (f32(PARAMS, SB_DEV, LANES), f32(AXES, KN)),
        [VMEM] * 5,
        name="final",
    )(row, z_src, w_src, z_att, w_att)
    return jnp.transpose(src, (1, 0, 2)), att


def solution(mesh):
    placed = (
        P(("src", "tm"), None, None),
        P(("src", "tm"), None, None),
        P(("src", "tm"), None),
        P(("src", "tm"), None),
        P(("src", "tm"), None),
        P(("src", "tm")),
        P(("src", "tm")),
        P(("src", "tm")),
        P(("src", "tm"), None),
    )
    return jax.shard_map(
        shards,
        mesh=mesh,
        in_specs=placed,
        out_specs=(P(("src", "tm"), None, None), P(None, "tm")),
        check_vma=False,
    )
```

```python
import functools

import jax
import jax.numpy as jnp
from jax import lax
from jax.experimental import pallas as pl
from jax.experimental.pallas import tpu as pltpu
from jax.sharding import PartitionSpec as P

KN = 4096
HW = 128
SB_DEV = 32
damping = 1.0

LANES = 128
ROWS = KN // LANES
AXES = 3
PART = AXES * ROWS + 8
PARAMS = 5
CAP = 8
EXTRA = PARAMS * CAP
PIECE = EXTRA + 8
UNROLL = 128
F32 = jnp.float32
BF16 = jnp.bfloat16


def place_of(axis, row):
    return axis * ROWS + row if row < ROWS else AXES * ROWS + axis


def iota(shape, dim):
    return lax.broadcasted_iota(jnp.int32, shape, dim)


def spline_weights(fraction):
    remain = 1.0 - fraction
    square = fraction * fraction
    cubed = square * fraction
    return (
        remain * remain * remain / 6.0,
        (3.0 * cubed - 6.0 * square + 4.0) / 6.0,
        (-3.0 * cubed + 3.0 * square + 3.0 * fraction + 1.0) / 6.0,
        cubed / 6.0,
    )


def split2(value):
    high = value.astype(BF16)
    return high, (value - high.astype(F32)).astype(BF16)


def split3(value):
    high, rest = value.astype(BF16), None
    rest = value - high.astype(F32)
    middle = rest.astype(BF16)
    return high, middle, (rest - middle.astype(F32)).astype(BF16)


def total(value):
    return jnp.sum(jnp.sum(value, axis=0, keepdims=True), axis=1, keepdims=True)


def row_of(ref, row):
    return jnp.broadcast_to(ref[pl.ds(row, 1), :], (8, LANES))


def places(t, offset_ref, knot_ref):
    place = row_of(knot_ref, t) + offset_ref[t] % LANES
    first = place < LANES
    return jnp.where(first, place, place - LANES), first


def add_adjoint(tiles, values, where, design, slot_ref, offset_ref, acc, knots):
    lane_row = iota((LANES, LANES), 0).astype(F32).astype(BF16)
    yes, no = jnp.ones((), BF16), jnp.zeros((), BF16)
    outs = []
    for t, resid, (lane, first) in zip(tiles, values, where):
        lane, first = lane[0:1], first[0:1]
        hot = jnp.where(lane_row == lane.astype(F32).astype(BF16), yes, no)
        high, low = split2(
            jnp.concatenate([design[t, 0:8, :] * resid, design[t, 8:16, :] * resid], axis=0)
        )
        here = jnp.broadcast_to(jnp.where(first, 1.0, 0.0).astype(BF16), high.shape)
        parts = (high * here, low * here)
        parts = parts + (high - parts[0], low - parts[1])
        outs.append(
            lax.dot_general(
                jnp.concatenate(parts, axis=0),
                hot,
                (((1,), (1,)), ((), ())),
                preferred_element_type=F32,
            )
        )
    for t, resid, out in zip(tiles, values, outs):
        slot = slot_ref[t]
        acc[slot] += design[t, 16:24, :] * resid
        row = offset_ref[t] // LANES
        knots[row] += out[0:16] + out[16:32]
        knots[row + 1] += out[32:48] + out[48:64]


def send_sums(acc, knots, piece_ref, att_ref, owners):
    for owner in range(owners):
        for param in range(PARAMS):
            piece_ref[owner * PIECE + param * CAP : owner * PIECE + param * CAP + CAP, :] = acc[
                owner * CAP : owner * CAP + CAP, param, :
            ]
    lane = iota((8, LANES), 1)
    low = iota((8, LANES), 0) < 4
    before = [jnp.zeros((8, LANES), F32)] * 3
    for row in range(ROWS + 1):
        one, two = knots[row, 0:8, :], knots[row, 8:16, :]
        now = [pltpu.roll(one, 1, 1), pltpu.roll(two, 2, 1), pltpu.roll(two, 3, 1)]
        moved = [jnp.where(lane >= k + 1, now[k], before[k]) for k in range(3)]
        both = jnp.where(low, one + moved[1], moved[0] + moved[2])
        both = both + pltpu.roll(both, 4, 0)
        for axis in range(AXES):
            at = place_of(axis, row)
            att_ref[at : at + 1, :] = both[axis : axis + 1]
        before = now


def first_kernel(
    slot_hbm,
    offset_hbm,
    valid_hbm,
    src_hbm,
    att_hbm,
    frac_hbm,
    knot_hbm,
    obs_hbm,
    table_hbm,
    design,
    piece_ref,
    part_ref,
    acc,
    knots,
    wts,
    slot_ref,
    offset_ref,
    valid_ref,
    src_ref,
    att_ref,
    frac_ref,
    knot_ref,
    obs_ref,
    table_ref,
    sems,
):
    pairs = (
        (frac_hbm, frac_ref),
        (offset_hbm, offset_ref),
        (valid_hbm, valid_ref),
        (slot_hbm, slot_ref),
        (knot_hbm, knot_ref),
        (obs_hbm, obs_ref),
        (att_hbm, att_ref),
        (src_hbm, src_ref.at[0 : src_hbm.shape[0]]),
        (table_hbm, table_ref),
    )
    copies = [pltpu.make_async_copy(a, b, sems.at[k]) for k, (a, b) in enumerate(pairs)]
    for copy in copies:
        copy.start()
    tiles = knot_ref.shape[0]
    owners = table_ref.shape[0]
    acc[...] = jnp.zeros_like(acc)
    knots[...] = jnp.zeros_like(knots)
    part_ref[...] = jnp.zeros_like(part_ref)
    for copy in copies:
        copy.wait()
    for k, weight in enumerate(spline_weights(frac_ref[...])):
        wts[k] = weight
    sub = iota((8, LANES), 0)
    lane = iota((8, LANES), 1)

    def body(step, carry):
        batch = [step * UNROLL + k for k in range(UNROLL)]
        for t in batch:
            live = lane < valid_ref[t]
            three = [row_of(att_ref, axis * tiles + t) for axis in range(AXES)]
            axis_of = sub % 4
            mixed = jnp.where(axis_of == 0, three[0], jnp.where(axis_of == 1, three[1], three[2]))
            mixed = jnp.where(live & (axis_of < 3), mixed, 0.0)
            weights = [row_of(wts.at[k], t) for k in range(4)]
            design[t, 0:8, :] = mixed * jnp.where(sub < 4, weights[0], weights[1])
            design[t, 8:16, :] = mixed * jnp.where(sub < 4, weights[2], weights[3])
            design[t, 16:24, :] = jnp.where(
                live & (sub < PARAMS), src_ref[pl.ds(t, 8, stride=tiles), :], 0.0
            )
        values = [row_of(obs_ref, t) for t in batch]
        where = [places(t, offset_ref, knot_ref) for t in batch]
        add_adjoint(batch, values, where, design, slot_ref, offset_ref, acc, knots)
        return carry

    lax.fori_loop(0, tiles // UNROLL, body, 0)
    send_sums(acc, knots, piece_ref, part_ref, owners)
    me = lax.axis_index("tm")
    placed = (iota((CAP, LANES), 1) == iota((CAP, LANES), 0) + me * CAP).astype(BF16)
    names = jnp.dot(
        table_ref[...].astype(F32).astype(BF16), placed, preferred_element_type=F32
    )
    for owner in range(owners):
        piece_ref[owner * PIECE + EXTRA : owner * PIECE + PIECE, :] = jnp.where(
            sub == 0, jnp.broadcast_to(names[owner : owner + 1], (8, LANES)), 0.0
        )


def att_kernel(*refs):
    level, out_ref = [part[...] for part in refs[:-1]], refs[-1]
    while len(level) > 1:
        level = [level[k] + level[k + 1] for k in range(0, len(level), 2)]
    out_ref[...] = level[0]


def owner_kernel(with_names, piece_ref, att_ref, *rest):
    if with_names:
        own_ref, back_ref, names_ref = rest
    else:
        names_in, own_in, own_ref, back_ref = rest
    owners = piece_ref.shape[0]
    rows = owners * CAP
    sub = iota((8, LANES), 0)
    if with_names:
        names = piece_ref[0, EXTRA : EXTRA + 8, :]
        for owner in range(1, owners):
            names = names + piece_ref[owner, EXTRA : EXTRA + 8, :]
        names_ref[...] = names
    else:
        names = names_in[...]
    hot = (iota((LANES, LANES), 0).astype(F32) == jnp.broadcast_to(names[0:1], (LANES, LANES))).astype(F32)
    pick = hot[0:SB_DEV, 0:rows].astype(BF16)
    give = hot.T[0:rows, 0:SB_DEV].astype(BF16)
    pick = jnp.concatenate([pick] * 3, axis=1)
    give = jnp.concatenate([give] * 3, axis=1)
    square = jnp.zeros((SB_DEV, LANES), F32)
    if not with_names:
        sums = piece_ref[0, EXTRA : EXTRA + 8, :]
        for owner in range(1, owners):
            sums = sums + piece_ref[owner, EXTRA : EXTRA + 8, :]
        sigma = sums[1:2, 0:1] / sums[1:2, 1:2]
        across = jnp.zeros((SB_DEV, LANES), F32)
    got = jnp.concatenate(
        [piece_ref[:, p * CAP : p * CAP + CAP, :].reshape(rows, LANES) for p in range(PARAMS)], axis=1
    )
    mine_all = jnp.dot(pick, jnp.concatenate(split3(got), axis=0), preferred_element_type=F32)
    back = jnp.dot(give, jnp.concatenate(split3(mine_all), axis=0), preferred_element_type=F32)
    for param in range(PARAMS):
        lanes = slice(param * LANES, param * LANES + LANES)
        mine = mine_all[:, lanes]
        own_ref[param] = mine
        back_ref[:, param * CAP : param * CAP + CAP, :] = back[:, lanes].reshape(owners, CAP, LANES)
        if with_names:
            square = square + mine * mine
        else:
            before = own_in[param]
            rest_ = mine - sigma * before
            square = square + rest_ * rest_
            across = across + rest_ * before
    extra = jnp.zeros((8, LANES), F32)
    for axis in range(AXES):
        for k, row in enumerate((0, ROWS)):
            at = place_of(axis, row)
            extra = jnp.where(sub == k * AXES + axis, att_ref[at : at + 1, :], extra)
    lane = iota((8, LANES), 1)
    numbers = jnp.where(lane == 0, total(square), 0.0)
    if not with_names:
        numbers = jnp.where(lane == 1, total(across), numbers)
        numbers = jnp.where(lane == 2, sigma, numbers)
        numbers = jnp.where(lane == 3, sums[1:2, 0:1], numbers)
        numbers = jnp.where(lane == 4, sums[1:2, 1:2], numbers)
    extra = jnp.where(sub == 2 * AXES, numbers, extra)
    for owner in range(owners):
        back_ref[owner, EXTRA : EXTRA + 8, :] = extra


def load_vector(got_ref, part_ref, slots, table, true_ref):
    owners = got_ref.shape[0] // PIECE
    me = lax.axis_index("tm")
    slots[...] = jnp.zeros_like(slots)
    for owner in range(owners):
        for param in range(PARAMS):
            slots[owner * CAP : owner * CAP + CAP, param, :] = got_ref[
                owner * PIECE + param * CAP : owner * PIECE + param * CAP + CAP, :
            ]
    left = got_ref[pl.ds(jnp.maximum(me - 1, 0) * PIECE + EXTRA, 8), :]
    right = got_ref[pl.ds(jnp.minimum(me + 1, owners - 1) * PIECE + EXTRA, 8), :]
    left = jnp.where(me > 0, left, 0.0)
    right = jnp.where(me < owners - 1, right, 0.0)
    has_right = jnp.where(me < owners - 1, 1.0, 0.0)
    sub = iota((8, LANES), 0)
    lane = iota((8, LANES), 1)
    low = sub < 4
    axis_of = sub % 4
    for axis in range(AXES):
        at = axis * ROWS
        true_ref[axis] = part_ref[at : at + ROWS, :]
        true_ref[axis, 0:1, :] = part_ref[at : at + 1, :] + left[AXES + axis : AXES + axis + 1]

    def mixed(row):
        if row < ROWS:
            three = [true_ref[axis, row : row + 1, :] for axis in range(AXES)]
        else:
            three = [
                right[axis : axis + 1] + has_right * part_ref[AXES * ROWS + axis : AXES * ROWS + axis + 1, :]
                for axis in range(AXES)
            ]
        three = [jnp.broadcast_to(v, (8, LANES)) for v in three]
        out = jnp.where(axis_of == 0, three[0], jnp.where(axis_of == 1, three[1], three[2]))
        return jnp.where(axis_of < 3, out, 0.0)

    def rolled(value):
        return [pltpu.roll(value, LANES - k, 1) for k in (1, 2, 3)]

    now = mixed(0)
    now_rolled = rolled(now)
    for row in range(ROWS + 1):
        after = mixed(row + 1) if row < ROWS else jnp.zeros((8, LANES), F32)
        after_rolled = rolled(after)
        moved = [jnp.where(lane < LANES - 1 - k, now_rolled[k], after_rolled[k]) for k in range(3)]
        table[row, 0:8, :] = jnp.where(low, now, moved[0])
        table[row, 8:16, :] = jnp.where(low, moved[1], moved[2])
        now, now_rolled = after, after_rolled


def forward(tiles, where, design, slot_ref, offset_ref, slots, table):
    values = []
    for t, (lane, first) in zip(tiles, where):
        row = offset_ref[t] // LANES
        summed = design[t, 16:24, :] * slots[slot_ref[t]]
        for half in (0, 8):
            here = jnp.take_along_axis(table[row, half : half + 8, :], lane, axis=1)
            there = jnp.take_along_axis(table[row + 1, half : half + 8, :], lane, axis=1)
            summed = summed + design[t, half : half + 8, :] * jnp.where(first, here, there)
        summed = summed + pltpu.roll(summed, 4, 0)
        summed = summed + pltpu.roll(summed, 2, 0)
        values.append(summed + pltpu.roll(summed, 1, 0))
    return values


def middle_kernel(
    copies,
    slot_ref,
    offset_ref,
    got_ref,
    part_ref,
    design,
    knot_ref,
    piece_ref,
    sum_ref,
    true_ref,
    y_ref,
    acc,
    knots,
    slots,
    table,
):
    tiles = design.shape[0]
    owners = got_ref.shape[0] // PIECE
    acc[...] = jnp.zeros_like(acc)
    knots[...] = jnp.zeros_like(knots)
    sum_ref[...] = jnp.zeros_like(sum_ref)
    load_vector(got_ref, part_ref, slots, table, true_ref)

    def body(step, carry):
        batch = [step * UNROLL + k for k in range(UNROLL)]
        where = [places(t, offset_ref, knot_ref) for t in batch]
        values = forward(batch, where, design, slot_ref, offset_ref, slots, table)
        for t, value in zip(batch, values):
            y_ref[pl.ds(t, 1), :] = value[0:1]
        add_adjoint(batch, values, where, design, slot_ref, offset_ref, acc, knots)
        return carry

    lax.fori_loop(0, tiles // UNROLL, body, 0)
    square = y_ref[...] * y_ref[...]
    send_sums(acc, knots, piece_ref, sum_ref, owners)
    norm_att = jnp.zeros((ROWS, LANES), F32)
    for axis in range(AXES):
        norm_att = norm_att + true_ref[axis] * true_ref[axis]
    me = lax.axis_index("tm")
    sent = got_ref[pl.ds(me * PIECE + EXTRA, 8), :]
    norm = sent[2 * AXES : 2 * AXES + 1, 0:1] + total(norm_att) / copies
    lane = iota((8, LANES), 1)
    numbers = jnp.where(lane == 0, total(square), jnp.where(lane == 1, norm, 0.0))
    numbers = jnp.where(iota((8, LANES), 0) == 1, numbers, 0.0)
    for owner in range(owners):
        piece_ref[owner * PIECE + EXTRA : owner * PIECE + PIECE, :] = numbers


def last_kernel(
    copies,
    slot_ref,
    offset_ref,
    got_ref,
    part_ref,
    design,
    knot_ref,
    y_ref,
    numbers_ref,
    before_ref,
    true_ref,
    out_ref,
    slots,
    table,
    after_ref,
):
    tiles = design.shape[0]
    owners = got_ref.shape[0] // PIECE
    load_vector(got_ref, part_ref, slots, table, true_ref)

    def body(step, carry):
        batch = [step * UNROLL + k for k in range(UNROLL)]
        where = [places(t, offset_ref, knot_ref) for t in batch]
        values = forward(batch, where, design, slot_ref, offset_ref, slots, table)
        for t, value in zip(batch, values):
            after_ref[pl.ds(t, 1), :] = value[0:1]
        return carry

    lax.fori_loop(0, tiles // UNROLL, body, 0)
    me = lax.axis_index("tm")
    sent = got_ref[pl.ds(me * PIECE + EXTRA, 8), :][2 * AXES : 2 * AXES + 1]
    group = got_ref[EXTRA : EXTRA + 8, :]
    for owner in range(1, owners):
        group = group + got_ref[owner * PIECE + EXTRA : owner * PIECE + EXTRA + 8, :]
    group = group[2 * AXES : 2 * AXES + 1]
    sigma, s_group, n_group = sent[:, 2:3], sent[:, 3:4], sent[:, 4:5]
    square_att = jnp.zeros((ROWS, LANES), F32)
    across_att = jnp.zeros((ROWS, LANES), F32)
    for axis in range(AXES):
        rest = true_ref[axis] - sigma * before_ref[axis]
        square_att = square_att + rest * rest
        across_att = across_att + rest * before_ref[axis]
    square_att = total(square_att) / copies
    across_att = total(across_att) / copies
    d_group = group[:, 0:1] + square_att * owners
    tau = sigma + d_group / (s_group + n_group)
    rest = after_ref[...] - tau * y_ref[...]
    square, across = rest * rest, rest * y_ref[...]
    own = numbers_ref[...][EXTRA + 1 : EXTRA + 2]
    numbers = [
        own[:, 1:2],
        own[:, 0:1],
        sent[:, 0:1] + square_att,
        sent[:, 1:2] + across_att,
        sigma,
        total(square),
        total(across),
        tau,
    ]
    lane = iota((1, LANES), 1)
    out = jnp.zeros((1, LANES), F32)
    for k, number in enumerate(numbers):
        out = jnp.where(lane == k, number, out)
    out_ref[...] = jnp.broadcast_to(out[None], out_ref.shape)


def final_kernel(got_ref, z_src, w_src, z_att, w_att, src_out, att_out):
    devices = got_ref.shape[0]
    got = got_ref[...].reshape(devices, LANES)

    def column(k):
        return got[:, k : k + 1]

    def summed(value):
        return jnp.sum(value, axis=0, keepdims=True)

    n_of, s_of = column(0), column(1)
    n, s = summed(n_of), summed(s_of)
    sigma = s / n
    alpha = n / (s + n)
    off = column(4) - sigma
    d = summed(column(2) + 2.0 * off * column(3) + off * off * n_of)
    gamma = alpha * d / n
    tau = sigma + gamma
    off = column(7) - tau
    e = summed(column(5) + 2.0 * off * column(6) + off * off * s_of)
    second = d / (e + damping * (d + gamma * gamma * n))
    c_z = alpha * (1.0 + second * tau)
    c_w = alpha * second
    for param in range(PARAMS):
        src_out[param] = c_z * z_src[param] - c_w * w_src[param]
    for axis in range(AXES):
        value = c_z * z_att[axis] - c_w * w_att[axis]
        for row in range(ROWS):
            att_out[axis : axis + 1, row * LANES : (row + 1) * LANES] = value[row : row + 1]


VMEM = pl.BlockSpec(memory_space=pltpu.VMEM)
SMEM = pl.BlockSpec(memory_space=pltpu.SMEM)
HBM = pl.BlockSpec(memory_space=pltpu.HBM)
PARAMETERS = pltpu.CompilerParams(vmem_limit_bytes=24 * 1024 * 1024)
HIDES = pl.CostEstimate(flops=0, bytes_accessed=64 * 1024 * 1024, transcendentals=0)


def f32(*shape):
    return jax.ShapeDtypeStruct(shape, F32)


def call(kernel, out_shape, in_specs, scratch=(), name=None, cost=None):
    return pl.pallas_call(
        kernel,
        out_shape=out_shape,
        in_specs=in_specs,
        out_specs=jax.tree.map(lambda _: VMEM, out_shape),
        scratch_shapes=list(scratch),
        compiler_params=PARAMETERS,
        cost_estimate=cost,
        name=name,
    )


def shards(
    src_design,
    att_design,
    obs_frac,
    obs_knot,
    observed,
    tile_slot,
    tile_offset,
    tile_valid,
    slot_block,
):
    tiles = src_design.shape[0]
    owners = lax.axis_size("tm")
    copies = lax.axis_size("src")
    devices = owners * copies
    slot_count = owners * CAP
    acc = pltpu.VMEM((slot_count, 8, LANES), F32)
    knots = pltpu.VMEM((ROWS + 1, 16, LANES), F32)
    piece = f32(owners * PIECE, LANES)
    part = f32(PART, LANES)
    true = f32(AXES, ROWS, LANES)

    def exchange(pieces):
        return lax.all_to_all(pieces.reshape(owners, PIECE, LANES), "tm", 0, 0, tiled=True)

    def att_sum(own):
        parts = [own] + [
            lax.ppermute(own, "src", [(i, i ^ k) for i in range(copies)]) for k in range(1, copies)
        ]
        return call(att_kernel, part, [VMEM] * copies, name="att", cost=HIDES)(*parts)

    src_rows = jnp.transpose(src_design, (1, 0, 2)).reshape(PARAMS * tiles, LANES)
    att_rows = jnp.transpose(att_design, (1, 0, 2)).reshape(AXES * tiles, LANES)
    inputs = (tile_slot, tile_offset, tile_valid, src_rows, att_rows, obs_frac, obs_knot, observed, slot_block)
    design, pieces, own = call(
        first_kernel,
        (f32(tiles, 24, LANES), piece, part),
        [HBM] * len(inputs),
        [acc, knots, pltpu.VMEM((4, tiles, LANES), F32)]
        + [pltpu.SMEM((tiles,), jnp.int32)] * 3
        + [pltpu.VMEM((8 * tiles, LANES), F32)]
        + [pltpu.VMEM(value.shape, value.dtype) for value in inputs[4:]]
        + [pltpu.SemaphoreType.DMA((len(inputs),))],
        "first",
    )(*[pltpu.with_memory_space_constraint(value, pltpu.HBM) for value in inputs])
    got, z_part = exchange(pieces), att_sum(own)
    z_src, back, names = call(
        functools.partial(owner_kernel, True),
        (f32(PARAMS, SB_DEV, LANES), f32(owners, PIECE, LANES), f32(8, LANES)),
        [VMEM] * 2,
        name="owner_first",
    )(got, z_part)
    got = exchange(back).reshape(owners * PIECE, LANES)
    pieces, own, z_att, y = call(
        functools.partial(middle_kernel, copies),
        (piece, part, true, f32(tiles, LANES)),
        [SMEM] * 2 + [VMEM] * 4,
        [acc, knots, acc, knots],
        "middle",
    )(tile_slot, tile_offset, got, z_part, design, obs_knot)
    numbers = pieces
    got, w_part = exchange(pieces), att_sum(own)
    w_src, back = call(
        functools.partial(owner_kernel, False),
        (f32(PARAMS, SB_DEV, LANES), f32(owners, PIECE, LANES)),
        [VMEM] * 4,
        name="owner_second",
    )(got, w_part, names, z_src)
    got = exchange(back).reshape(owners * PIECE, LANES)
    w_att, row = call(
        functools.partial(last_kernel, copies),
        (true, f32(devices, 1, LANES)),
        [SMEM] * 2 + [VMEM] * 7,
        [acc, knots, pltpu.VMEM((tiles, LANES), F32)],
        "last",
    )(tile_slot, tile_offset, got, w_part, design, obs_knot, y, numbers, z_att)
    row = lax.all_to_all(row, ("src", "tm"), 0, 0, tiled=True)
    src, att = call(
        final_kernel,
        (f32(PARAMS, SB_DEV, LANES), f32(AXES, KN)),
        [VMEM] * 5,
        name="final",
    )(row, z_src, w_src, z_att, w_att)
    return jnp.transpose(src, (1, 0, 2)), att


def solution(mesh):
    placed = (
        P(("src", "tm"), None, None),
        P(("src", "tm"), None, None),
        P(("src", "tm"), None),
        P(("src", "tm"), None),
        P(("src", "tm"), None),
        P(("src", "tm")),
        P(("src", "tm")),
        P(("src", "tm")),
        P(("src", "tm"), None),
    )
    return jax.shard_map(
        shards,
        mesh=mesh,
        in_specs=placed,
        out_specs=(P(("src", "tm"), None, None), P(None, "tm")),
        check_vma=False,
    )
```

```python
import functools

import jax
import jax.numpy as jnp
from jax import lax
from jax.experimental import pallas as pl
from jax.experimental.pallas import tpu as pltpu
from jax.sharding import PartitionSpec as P

KN = 4096
HW = 128
SB_DEV = 32
damping = 1.0

LANES = 128
ROWS = KN // LANES
ROWS_PAD = (ROWS + 8) // 8 * 8
AXES = 3
PARAMS = 5
CAP = 8
UNROLL = 128
F32 = jnp.float32
BF16 = jnp.bfloat16


def iota(shape, dim):
    return lax.broadcasted_iota(jnp.int32, shape, dim)


def spline_weights(fraction):
    remain = 1.0 - fraction
    square = fraction * fraction
    cubed = square * fraction
    return (
        remain * remain * remain / 6.0,
        (3.0 * cubed - 6.0 * square + 4.0) / 6.0,
        (-3.0 * cubed + 3.0 * square + 3.0 * fraction + 1.0) / 6.0,
        cubed / 6.0,
    )


def split2(value):
    high = value.astype(BF16)
    return high, (value - high.astype(F32)).astype(BF16)


def split3(value):
    high, rest = value.astype(BF16), None
    rest = value - high.astype(F32)
    middle = rest.astype(BF16)
    return high, middle, (rest - middle.astype(F32)).astype(BF16)


def total(value):
    return jnp.sum(jnp.sum(value, axis=0, keepdims=True), axis=1, keepdims=True)


def row_of(ref, row):
    return jnp.broadcast_to(ref[pl.ds(row, 1), :], (8, LANES))


def add_adjoint(tiles, values, design, offset_ref, knot_ref, knots):
    lane_row = iota((LANES, LANES), 0).astype(F32).astype(BF16)
    yes, no = jnp.ones((), BF16), jnp.zeros((), BF16)
    outs = []
    for t, resid in zip(tiles, values):
        shift = offset_ref[t] % LANES
        place = knot_ref[pl.ds(t, 1), :] + shift
        first = place < LANES
        lane = jnp.where(first, place, place - LANES)
        hot = jnp.where(lane_row == lane.astype(F32).astype(BF16), yes, no)
        high, low = split2(
            jnp.concatenate([design[t, 0:8, :] * resid, design[t, 8:16, :] * resid], axis=0)
        )
        here = jnp.broadcast_to(jnp.where(first, 1.0, 0.0).astype(BF16), high.shape)
        parts = (high * here, low * here)
        parts = parts + (high - parts[0], low - parts[1])
        outs.append(
            lax.dot_general(
                jnp.concatenate(parts, axis=0),
                hot,
                (((1,), (1,)), ((), ())),
                preferred_element_type=F32,
            )
        )
    for t, out in zip(tiles, outs):
        row = offset_ref[t] // LANES
        knots[row] += out[0:16] + out[16:32]
        knots[row + 1] += out[32:48] + out[48:64]


def send_sums(knots, att_ref, rim_ref):
    lane = iota((8, LANES), 1)
    low = iota((8, LANES), 0) < 4
    before = [jnp.zeros((8, LANES), F32)] * 3
    for row in range(ROWS + 1):
        one, two = knots[row, 0:8, :], knots[row, 8:16, :]
        now = [pltpu.roll(one, 1, 1), pltpu.roll(two, 2, 1), pltpu.roll(two, 3, 1)]
        moved = [jnp.where(lane >= k + 1, now[k], before[k]) for k in range(3)]
        both = jnp.where(low, one + moved[1], moved[0] + moved[2])
        both = both + pltpu.roll(both, 4, 0)
        for axis in range(AXES):
            att_ref[axis * ROWS_PAD + row : axis * ROWS_PAD + row + 1, :] = both[axis : axis + 1]
        if row == 0:
            rim_ref[...] = both
        before = now
    moved = pltpu.roll(both, 4, 0)
    rim_ref[...] = jnp.where(low, rim_ref[...], moved)


def first_kernel(
    offset_hbm,
    valid_hbm,
    att_hbm,
    frac_hbm,
    knot_hbm,
    obs_hbm,
    design,
    part_ref,
    rim_ref,
    knots,
    wts,
    offset_ref,
    valid_ref,
    att_ref,
    frac_ref,
    knot_ref,
    obs_ref,
    sems,
):
    pairs = (
        (frac_hbm, frac_ref),
        (offset_hbm, offset_ref),
        (valid_hbm, valid_ref),
        (knot_hbm, knot_ref),
        (obs_hbm, obs_ref),
        (att_hbm, att_ref),
    )
    copies = [pltpu.make_async_copy(a, b, sems.at[k]) for k, (a, b) in enumerate(pairs)]
    for copy in copies:
        copy.start()
    tiles = knot_ref.shape[0]
    knots[...] = jnp.zeros_like(knots)
    part_ref[...] = jnp.zeros_like(part_ref)
    for copy in copies:
        copy.wait()
    for k, weight in enumerate(spline_weights(frac_ref[...])):
        wts[k] = weight
    sub = iota((8, LANES), 0)
    lane = iota((8, LANES), 1)
    axis_of = sub % 4

    def body(step, carry):
        batch = [step * UNROLL + k for k in range(UNROLL)]
        for t in batch:
            live = lane < valid_ref[t]
            three = [row_of(att_ref, axis * tiles + t) for axis in range(AXES)]
            mixed = jnp.where(axis_of == 0, three[0], jnp.where(axis_of == 1, three[1], three[2]))
            mixed = jnp.where(live & (axis_of < 3), mixed, 0.0)
            weights = [row_of(wts.at[k], t) for k in range(4)]
            design[t, 0:8, :] = mixed * jnp.where(sub < 4, weights[0], weights[1])
            design[t, 8:16, :] = mixed * jnp.where(sub < 4, weights[2], weights[3])
        values = [row_of(obs_ref, t) for t in batch]
        add_adjoint(batch, values, design, offset_ref, knot_ref, knots)
        return carry

    lax.fori_loop(0, tiles // UNROLL, body, 0)
    send_sums(knots, part_ref, rim_ref)


def send_slots(acc, piece_ref, extra):
    slots = acc.shape[0]
    for param in range(PARAMS):
        for at in range(0, slots, 8):
            piece_ref[param * slots + at : param * slots + at + 8, :] = acc[at : at + 8, param, :]
    piece_ref[PARAMS * slots :, :] = extra


def first_sources(
    slot_ref, valid_ref, src_ref, obs_ref, table_ref, after_ref, design, piece_ref, acc
):
    del after_ref
    tiles = obs_ref.shape[0]
    owners = table_ref.shape[0]
    acc[...] = jnp.zeros_like(acc)
    lane = iota((PARAMS, LANES), 1)
    zero = jnp.zeros((8, LANES), F32)

    def body(step, carry):
        for k in range(UNROLL):
            t = step * UNROLL + k
            rows = jnp.where(lane < valid_ref[t], src_ref[pl.ds(t, PARAMS, stride=tiles), :], 0.0)
            design[t] = zero
            design[t, 0:PARAMS, :] = rows
            acc[slot_ref[t], 0:PARAMS, :] += rows * row_of(obs_ref, t)[0:PARAMS]
        return carry

    lax.fori_loop(0, tiles // UNROLL, body, 0)
    col = iota((CAP, LANES), 1)
    placed = (col % CAP == iota((CAP, LANES), 0)).astype(BF16)
    names = jnp.dot(table_ref[...].astype(F32).astype(BF16), placed, preferred_element_type=F32)
    col = iota((owners, LANES), 1)
    owner = iota((owners, LANES), 0)
    names = jnp.where(col // CAP == owner, names + (owner * SB_DEV).astype(F32), 0.0)
    names = jnp.sum(names, axis=0, keepdims=True)
    names = jnp.where(iota((8, LANES), 0) == 0, jnp.broadcast_to(names, (8, LANES)), 0.0)
    send_slots(acc, piece_ref, names)


def later_sources(slot_ref, design, y_ref, numbers_ref, piece_ref, acc):
    tiles = y_ref.shape[0]
    acc[...] = jnp.zeros_like(acc)

    def body(step, carry):
        for k in range(UNROLL):
            t = step * UNROLL + k
            acc[slot_ref[t]] += design[t] * row_of(y_ref, t)
        return carry

    lax.fori_loop(0, tiles // UNROLL, body, 0)
    send_slots(acc, piece_ref, numbers_ref[...])


def att_kernel(*refs):
    level, out_ref = [part[...] for part in refs[:-1]], refs[-1]
    while len(level) > 1:
        level = [level[k] + level[k + 1] for k in range(0, len(level), 2)]
    out_ref[...] = level[0]


def rim_kernel(part_ref, near_ref, far_ref, out_ref):
    owners = lax.axis_size("tm")
    me = lax.axis_index("tm")
    even = jnp.full((8, LANES), me % 2, jnp.int32) == 0
    near, far = near_ref[...], far_ref[...]
    left = jnp.where(me > 0, jnp.where(even, far, near), 0.0)
    right = jnp.where(me < owners - 1, jnp.where(even, near, far), 0.0)
    has_right = jnp.where(me < owners - 1, 1.0, 0.0)
    out_ref[...] = part_ref[...]
    for axis in range(AXES):
        at = axis * ROWS_PAD
        out_ref[at : at + 1, :] = part_ref[at : at + 1, :] + left[4 + axis : 5 + axis]
        at = at + ROWS
        out_ref[at : at + 1, :] = has_right * part_ref[at : at + 1, :] + right[axis : axis + 1]


def dense_kernel(slots, with_names, *refs):
    if with_names:
        refs, names_out = refs[:-1], refs[-1]
    else:
        names_in, refs = refs[0], refs[1:]
    pieces, dense_ref = refs[:-2], refs[-1]
    blocks = (dense_ref.shape[0] - 8) // PARAMS
    last = PARAMS * slots
    extras = [piece[last : last + 8, :] for piece in pieces]
    if with_names:
        names = [extra[0:1] for extra in extras]
        out = jnp.zeros(names_out.shape, F32)
        for k, name in enumerate(names):
            out = jnp.where(iota(out.shape, 0) == k, jnp.broadcast_to(name, out.shape), out)
        names_out[...] = out
    else:
        names = [names_in[k : k + 1, :] for k in range(len(pieces))]
    block = iota((blocks, slots), 0).astype(F32)
    hot = jnp.concatenate(
        [
            jnp.where(block == jnp.broadcast_to(name[:, 0:slots], block.shape), 1.0, 0.0).astype(BF16)
            for name in names
        ],
        axis=1,
    )
    got = jnp.concatenate(
        [
            jnp.concatenate([piece[p * slots : p * slots + slots, :] for piece in pieces], axis=0)
            for p in range(PARAMS)
        ],
        axis=1,
    )
    three = [jnp.dot(hot, part, preferred_element_type=F32) for part in split3(got)]
    summed = (three[2] + three[1]) + three[0]
    for param in range(PARAMS):
        dense_ref[param * blocks : param * blocks + blocks, :] = summed[:, param * LANES : (param + 1) * LANES]
    numbers = extras[0]
    for extra in extras[1:]:
        numbers = numbers + extra
    dense_ref[PARAMS * blocks :, :] = numbers


def load_vector(mine_ref, other_ref, parts, dense, table, true_ref, own_ref):
    rows = mine_ref.shape[0] - 8
    blocks = rows // PARAMS
    me = lax.axis_index("tm")
    dense[0:rows, :] = mine_ref[0:rows, :] + other_ref[0:rows, :]
    dense[rows:, :] = jnp.zeros((dense.shape[0] - rows, LANES), F32)
    for param in range(PARAMS):
        at = pl.multiple_of(param * blocks + me * SB_DEV, SB_DEV)
        own_ref[param] = dense[pl.ds(at, SB_DEV), :]
    sub = iota((8, LANES), 0)
    lane = iota((8, LANES), 1)
    low = sub < 4
    axis_of = sub % 4
    level = [part[...] for part in parts]
    while len(level) > 1:
        level = [level[k] + level[k + 1] for k in range(0, len(level), 2)]
    att = level[0]
    for axis in range(AXES):
        true_ref[axis] = att[axis * ROWS_PAD : axis * ROWS_PAD + ROWS]

    def mixed(row):
        three = [att[axis * ROWS_PAD + row : axis * ROWS_PAD + row + 1] for axis in range(AXES)]
        three = [jnp.broadcast_to(v, (8, LANES)) for v in three]
        out = jnp.where(axis_of == 0, three[0], jnp.where(axis_of == 1, three[1], three[2]))
        return jnp.where(axis_of < 3, out, 0.0)

    def rolled(value):
        return [pltpu.roll(value, LANES - k, 1) for k in (1, 2, 3)]

    now = mixed(0)
    now_rolled = rolled(now)
    for row in range(ROWS + 1):
        after = mixed(row + 1) if row < ROWS else jnp.zeros((8, LANES), F32)
        after_rolled = rolled(after)
        moved = [jnp.where(lane < LANES - 1 - k, now_rolled[k], after_rolled[k]) for k in range(3)]
        table[row, 0:8, :] = jnp.where(low, now, moved[0])
        table[row, 8:16, :] = jnp.where(low, moved[1], moved[2])
        now, now_rolled = after, after_rolled


def forward(tiles, design, sources, slot_ref, offset_ref, block_ref, knot_ref, dense, table):
    blocks = dense.shape[0] // 8
    values = []
    for t in tiles:
        shift = offset_ref[t] % LANES
        row = offset_ref[t] // LANES
        slot = slot_ref[t]
        block = slot // CAP * SB_DEV + block_ref[slot // CAP, slot % CAP]
        place = row_of(knot_ref, t) + shift
        first = place < LANES
        lane = jnp.where(first, place, place - LANES)
        summed = sources[t] * dense[pl.ds(block, 8, stride=blocks), :]
        for half in (0, 8):
            here = jnp.take_along_axis(table[row, half : half + 8, :], lane, axis=1)
            there = jnp.take_along_axis(table[row + 1, half : half + 8, :], lane, axis=1)
            summed = summed + design[t, half : half + 8, :] * jnp.where(first, here, there)
        summed = summed + pltpu.roll(summed, 4, 0)
        summed = summed + pltpu.roll(summed, 2, 0)
        values.append(summed + pltpu.roll(summed, 1, 0))
    return values


def middle_kernel(
    copies,
    slot_ref,
    offset_ref,
    block_ref,
    mine_ref,
    other_ref,
    design,
    sources,
    knot_ref,
    *refs,
):
    parts = refs[:1]
    numbers_ref, sum_ref, rim_ref, true_ref, own_ref, y_ref, knots, dense, table = refs[1:]
    tiles = design.shape[0]
    knots[...] = jnp.zeros_like(knots)
    sum_ref[...] = jnp.zeros_like(sum_ref)
    load_vector(mine_ref, other_ref, parts, dense, table, true_ref, own_ref)

    def body(step, square):
        batch = [step * UNROLL + k for k in range(UNROLL)]
        values = forward(batch, design, sources, slot_ref, offset_ref, block_ref, knot_ref, dense, table)
        for t, value in zip(batch, values):
            y_ref[pl.ds(t, 1), :] = value[0:1]
            square = square + value * value
        add_adjoint(batch, values, design, offset_ref, knot_ref, knots)
        return square

    square = lax.fori_loop(0, tiles // UNROLL, body, jnp.zeros((8, LANES), F32))
    send_sums(knots, sum_ref, rim_ref)
    norm_att = true_ref[0] * true_ref[0]
    for axis in range(1, AXES):
        norm_att = norm_att + true_ref[axis] * true_ref[axis]
    norm_src = own_ref[0] * own_ref[0]
    for param in range(1, PARAMS):
        norm_src = norm_src + own_ref[param] * own_ref[param]
    norm = total(norm_src) + total(norm_att) / copies
    lane = iota((8, LANES), 1)
    numbers = jnp.where(lane == 0, total(square[0:1]), jnp.where(lane == 1, norm, 0.0))
    numbers_ref[...] = jnp.where(iota((8, LANES), 0) == 1, numbers, 0.0)


def last_kernel(
    copies,
    slot_ref,
    offset_ref,
    block_ref,
    mine_ref,
    other_ref,
    design,
    sources,
    knot_ref,
    y_ref,
    numbers_ref,
    z_att,
    z_src,
    *refs,
):
    parts = refs[:1]
    true_ref, own_ref, out_ref, dense, table = refs[1:]
    tiles = design.shape[0]
    rows = mine_ref.shape[0] - 8
    owners = rows // (PARAMS * SB_DEV)
    load_vector(mine_ref, other_ref, parts, dense, table, true_ref, own_ref)
    group = (mine_ref[rows:, :] + other_ref[rows:, :])[1:2]
    s_group, n_group = group[:, 0:1], group[:, 1:2]
    sigma = s_group / n_group

    def about(new, old, count):
        square, across = None, None
        for k in range(count):
            rest = new[k] - sigma * old[k]
            first, second = rest * rest, rest * old[k]
            square = first if square is None else square + first
            across = second if across is None else across + second
        return total(square), total(across)

    att, src = about(true_ref, z_att, AXES), about(own_ref, z_src, PARAMS)
    d_square = src[0] + att[0] / copies
    d_across = src[1] + att[1] / copies
    tau = sigma + owners * d_square / (s_group + n_group)
    tau_full = jnp.broadcast_to(tau, (8, LANES))

    def body(step, carry):
        square, across = carry
        batch = [step * UNROLL + k for k in range(UNROLL)]
        values = forward(batch, design, sources, slot_ref, offset_ref, block_ref, knot_ref, dense, table)
        for t, value in zip(batch, values):
            before = row_of(y_ref, t)
            rest = value - tau_full * before
            square = square + rest * rest
            across = across + rest * before
        return square, across

    zero = jnp.zeros((8, LANES), F32)
    square, across = lax.fori_loop(0, tiles // UNROLL, body, (zero, zero))
    own = numbers_ref[1:2, :]
    numbers = [
        own[:, 1:2],
        own[:, 0:1],
        d_square,
        d_across,
        sigma,
        total(square[0:1]),
        total(across[0:1]),
        tau,
    ]
    lane = iota((1, LANES), 1)
    out = jnp.zeros((1, LANES), F32)
    for k, number in enumerate(numbers):
        out = jnp.where(lane == k, number, out)
    out_ref[...] = jnp.broadcast_to(out[None], out_ref.shape)


def final_kernel(got_ref, z_src, w_src, z_att, w_att, src_out, att_out):
    devices = got_ref.shape[0]
    got = got_ref[...].reshape(devices, LANES)

    def column(k):
        return got[:, k : k + 1]

    def summed(value):
        return jnp.sum(value, axis=0, keepdims=True)

    n_of, s_of = column(0), column(1)
    n, s = summed(n_of), summed(s_of)
    sigma = s / n
    alpha = n / (s + n)
    off = column(4) - sigma
    d = summed(column(2) + 2.0 * off * column(3) + off * off * n_of)
    gamma = alpha * d / n
    tau = sigma + gamma
    off = column(7) - tau
    e = summed(column(5) + 2.0 * off * column(6) + off * off * s_of)
    second = d / (e + damping * (d + gamma * gamma * n))
    c_z = alpha * (1.0 + second * tau)
    c_w = alpha * second
    for param in range(PARAMS):
        src_out[param] = c_z * z_src[param] - c_w * w_src[param]
    for axis in range(AXES):
        value = c_z * z_att[axis] - c_w * w_att[axis]
        for row in range(ROWS):
            att_out[axis : axis + 1, row * LANES : (row + 1) * LANES] = value[row : row + 1]


VMEM = pl.BlockSpec(memory_space=pltpu.VMEM)
ANY = pl.BlockSpec(memory_space=pl.ANY)
SMEM = pl.BlockSpec(memory_space=pltpu.SMEM)
HBM = pl.BlockSpec(memory_space=pltpu.HBM)
MIB = 1024 * 1024


HIDES = pl.CostEstimate(flops=3 * 10**10, bytes_accessed=0, transcendentals=0)


def f32(*shape):
    return jax.ShapeDtypeStruct(shape, F32)


def call(kernel, out_shape, in_specs, scratch=(), name=None, grant=16, cost=None):
    return pl.pallas_call(
        kernel,
        out_shape=out_shape,
        in_specs=in_specs,
        out_specs=jax.tree.map(lambda _: VMEM, out_shape),
        scratch_shapes=list(scratch),
        compiler_params=pltpu.CompilerParams(vmem_limit_bytes=grant * MIB),
        cost_estimate=cost,
        name=name,
    )


def shards(
    src_design,
    att_design,
    obs_frac,
    obs_knot,
    observed,
    tile_slot,
    tile_offset,
    tile_valid,
    slot_block,
):
    tiles = src_design.shape[0]
    owners = lax.axis_size("tm")
    copies = lax.axis_size("src")
    devices = owners * copies
    slots = owners * CAP
    blocks = owners * SB_DEV
    acc = pltpu.VMEM((slots, 8, LANES), F32)
    knots = pltpu.VMEM((ROWS + 1, 16, LANES), F32)
    dense = pltpu.VMEM((8 * blocks, LANES), F32)
    piece = f32(PARAMS * slots + 8, LANES)
    summed = f32(PARAMS * blocks + 8, LANES)
    part = f32(AXES * ROWS_PAD, LANES)
    true = f32(AXES, ROWS, LANES)
    mine = f32(PARAMS, SB_DEV, LANES)
    rim = f32(8, LANES)

    def flipped(value, axis, bits):
        size = lax.axis_size(axis)
        return lax.ppermute(value, axis, [(i, i ^ bits) for i in range(size)])

    def att_sums(own, rims):
        near = flipped(rims, "tm", 1)
        route = [(i, i + 1) for i in range(1, owners - 1, 2)]
        far = lax.ppermute(rims, "tm", route + [(j, i) for i, j in route])
        own = call(rim_kernel, part, [VMEM] * 3, name="rims")(own, near, far)
        parts = [own] + [flipped(own, "src", k) for k in range(1, copies)]
        return own, call(att_kernel, part, [VMEM] * copies, name="att", cost=HIDES)(*parts)

    def src_sums(pieces, names, after):
        sent = [pieces] + [flipped(pieces, "tm", k) for k in range(2, owners, 2)]
        count = owners // 2
        if names is None:
            half, names = call(
                functools.partial(dense_kernel, slots, True),
                (summed, f32((count + 7) // 8 * 8, LANES)),
                [VMEM] * count + [ANY],
                name="dense_first",
            )(*sent, after)
        else:
            half = call(
                functools.partial(dense_kernel, slots, False),
                summed,
                [VMEM] * (1 + count) + [ANY],
                name="dense_second",
            )(names, *sent, after)
        return half, flipped(half, "tm", 1), names

    src_rows = jnp.transpose(src_design, (1, 0, 2)).reshape(PARAMS * tiles, LANES)
    att_rows = jnp.transpose(att_design, (1, 0, 2)).reshape(AXES * tiles, LANES)
    whole = (tiles, LANES)
    design, own, rims = call(
        first_kernel,
        (f32(tiles, 16, LANES), part, rim),
        [HBM] * 6,
        [
            knots,
            pltpu.VMEM((4, tiles, LANES), F32),
            pltpu.SMEM((tiles,), jnp.int32),
            pltpu.SMEM((tiles,), jnp.int32),
            pltpu.VMEM((AXES * tiles, LANES), F32),
            pltpu.VMEM(whole, F32),
            pltpu.VMEM(whole, jnp.int32),
            pltpu.VMEM(whole, F32),
            pltpu.SemaphoreType.DMA((6,)),
        ],
        "first",
    )(*[
        pltpu.with_memory_space_constraint(value, pltpu.HBM)
        for value in (tile_offset, tile_valid, att_rows, obs_frac, obs_knot, observed)
    ])
    sources, pieces = call(
        first_sources,
        (f32(tiles, 8, LANES), piece),
        [SMEM] * 2 + [VMEM] * 3 + [ANY],
        [acc],
        "first_sources",
    )(tile_slot, tile_valid, src_rows, observed, slot_block, own)
    own, att = att_sums(own, rims)
    half, other, names = src_sums(pieces, None, own)
    numbers, own, rims, z_att, z_src, y = call(
        functools.partial(middle_kernel, copies),
        (rim, part, rim, true, mine, f32(tiles, LANES)),
        [SMEM] * 3 + [VMEM] * 6,
        [knots, dense, knots],
        "middle",
    )(tile_slot, tile_offset, slot_block, half, other, design, sources, obs_knot, att)
    pieces = call(
        later_sources,
        piece,
        [SMEM] + [VMEM] * 3,
        [acc],
        "later_sources",
    )(tile_slot, sources, y, numbers)
    own, att = att_sums(own, rims)
    half, other, names = src_sums(pieces, names, own)
    w_att, w_src, row = call(
        functools.partial(last_kernel, copies),
        (true, mine, f32(devices, 1, LANES)),
        [SMEM] * 3 + [VMEM] * 10,
        [dense, knots],
        "last",
    )(
        tile_slot, tile_offset, slot_block, half, other, design, sources, obs_knot, y, numbers, z_att, z_src, att
    )
    row = lax.all_to_all(row, ("src", "tm"), 0, 0, tiled=True)
    src, att = call(
        final_kernel,
        (mine, f32(AXES, KN)),
        [VMEM] * 5,
        name="final",
    )(row, z_src, w_src, z_att, w_att)
    return jnp.transpose(src, (1, 0, 2)), att


def solution(mesh):
    placed = (
        P(("src", "tm"), None, None),
        P(("src", "tm"), None, None),
        P(("src", "tm"), None),
        P(("src", "tm"), None),
        P(("src", "tm"), None),
        P(("src", "tm")),
        P(("src", "tm")),
        P(("src", "tm")),
        P(("src", "tm"), None),
    )
    return jax.shard_map(
        shards,
        mesh=mesh,
        in_specs=placed,
        out_specs=(P(("src", "tm"), None, None), P(None, "tm")),
        check_vma=False,
    )
```

```python
import functools

import jax
import jax.numpy as jnp
from jax import lax
from jax.experimental import pallas as pl
from jax.experimental.pallas import tpu as pltpu
from jax.sharding import PartitionSpec as P

KN = 4096
HW = 128
SB_DEV = 32
damping = 1.0

LANES = 128
ROWS = KN // LANES
ROWS_PAD = (ROWS + 8) // 8 * 8
AXES = 3
PARAMS = 5
CAP = 8
UNROLL = 128
F32 = jnp.float32
BF16 = jnp.bfloat16


def iota(shape, dim):
    return lax.broadcasted_iota(jnp.int32, shape, dim)


def spline_weights(fraction):
    remain = 1.0 - fraction
    square = fraction * fraction
    cubed = square * fraction
    return (
        remain * remain * remain / 6.0,
        (3.0 * cubed - 6.0 * square + 4.0) / 6.0,
        (-3.0 * cubed + 3.0 * square + 3.0 * fraction + 1.0) / 6.0,
        cubed / 6.0,
    )


def split2(value):
    high = value.astype(BF16)
    return high, (value - high.astype(F32)).astype(BF16)


def split3(value):
    high, rest = value.astype(BF16), None
    rest = value - high.astype(F32)
    middle = rest.astype(BF16)
    return high, middle, (rest - middle.astype(F32)).astype(BF16)


def total(value):
    return jnp.sum(jnp.sum(value, axis=0, keepdims=True), axis=1, keepdims=True)


def row_of(ref, row):
    return jnp.broadcast_to(ref[pl.ds(row, 1), :], (8, LANES))


def places(t, offset_ref, knot_ref):
    place = row_of(knot_ref, t) + offset_ref[t] % LANES
    first = place < LANES
    return jnp.where(first, place, place - LANES), first


def add_adjoint(tiles, values, where, design, offset_ref, knots):
    lane_row = iota((LANES, LANES), 0).astype(F32).astype(BF16)
    yes, no = jnp.ones((), BF16), jnp.zeros((), BF16)
    outs = []
    for t, resid, (lane, first) in zip(tiles, values, where):
        lane, first = lane[0:1], first[0:1]
        hot = jnp.where(lane_row == lane.astype(F32).astype(BF16), yes, no)
        high, low = split2(
            jnp.concatenate([design[t, 0:8, :] * resid, design[t, 8:16, :] * resid], axis=0)
        )
        here = jnp.broadcast_to(jnp.where(first, 1.0, 0.0).astype(BF16), high.shape)
        parts = (high * here, low * here)
        parts = parts + (high - parts[0], low - parts[1])
        outs.append(
            lax.dot_general(
                jnp.concatenate(parts, axis=0),
                hot,
                (((1,), (1,)), ((), ())),
                preferred_element_type=F32,
            )
        )
    for t, out in zip(tiles, outs):
        row = offset_ref[t] // LANES
        knots[row] += out[0:16] + out[16:32]
        knots[row + 1] += out[32:48] + out[48:64]


def send_sums(knots, att_ref, rim_ref):
    lane = iota((8, LANES), 1)
    low = iota((8, LANES), 0) < 4
    before = [jnp.zeros((8, LANES), F32)] * 3
    for row in range(ROWS + 1):
        one, two = knots[row, 0:8, :], knots[row, 8:16, :]
        now = [pltpu.roll(one, 1, 1), pltpu.roll(two, 2, 1), pltpu.roll(two, 3, 1)]
        moved = [jnp.where(lane >= k + 1, now[k], before[k]) for k in range(3)]
        both = jnp.where(low, one + moved[1], moved[0] + moved[2])
        both = both + pltpu.roll(both, 4, 0)
        for axis in range(AXES):
            att_ref[axis * ROWS_PAD + row : axis * ROWS_PAD + row + 1, :] = both[axis : axis + 1]
        if row == 0:
            rim_ref[...] = both
        before = now
    moved = pltpu.roll(both, 4, 0)
    rim_ref[...] = jnp.where(low, rim_ref[...], moved)


def first_kernel(
    offset_hbm,
    valid_hbm,
    att_hbm,
    frac_hbm,
    knot_hbm,
    obs_hbm,
    design,
    part_ref,
    rim_ref,
    knots,
    wts,
    offset_ref,
    valid_ref,
    att_ref,
    frac_ref,
    knot_ref,
    obs_ref,
    sems,
):
    pairs = (
        (frac_hbm, frac_ref),
        (offset_hbm, offset_ref),
        (valid_hbm, valid_ref),
        (knot_hbm, knot_ref),
        (obs_hbm, obs_ref),
        (att_hbm, att_ref),
    )
    copies = [pltpu.make_async_copy(a, b, sems.at[k]) for k, (a, b) in enumerate(pairs)]
    for copy in copies:
        copy.start()
    tiles = knot_ref.shape[0]
    knots[...] = jnp.zeros_like(knots)
    part_ref[...] = jnp.zeros_like(part_ref)
    for copy in copies:
        copy.wait()
    for k, weight in enumerate(spline_weights(frac_ref[...])):
        wts[k] = weight
    sub = iota((8, LANES), 0)
    lane = iota((8, LANES), 1)
    axis_of = sub % 4

    def body(step, carry):
        batch = [step * UNROLL + k for k in range(UNROLL)]
        for t in batch:
            live = lane < valid_ref[t]
            three = [row_of(att_ref, axis * tiles + t) for axis in range(AXES)]
            mixed = jnp.where(axis_of == 0, three[0], jnp.where(axis_of == 1, three[1], three[2]))
            mixed = jnp.where(live & (axis_of < 3), mixed, 0.0)
            weights = [row_of(wts.at[k], t) for k in range(4)]
            design[t, 0:8, :] = mixed * jnp.where(sub < 4, weights[0], weights[1])
            design[t, 8:16, :] = mixed * jnp.where(sub < 4, weights[2], weights[3])
        values = [row_of(obs_ref, t) for t in batch]
        where = [places(t, offset_ref, knot_ref) for t in batch]
        add_adjoint(batch, values, where, design, offset_ref, knots)
        return carry

    lax.fori_loop(0, tiles // UNROLL, body, 0)
    send_sums(knots, part_ref, rim_ref)


def begin_copies(pairs, sems):
    copies = [pltpu.make_async_copy(a, b, sems.at[k]) for k, (a, b) in enumerate(pairs)]
    for copy in copies:
        copy.start()
    return copies


def send_slots(acc, piece_ref, extra):
    slots = acc.shape[0]
    for param in range(PARAMS):
        for at in range(0, slots, 8):
            piece_ref[param * slots + at : param * slots + at + 8, :] = acc[at : at + 8, param, :]
    piece_ref[PARAMS * slots :, :] = extra


def first_sources(
    slot_hbm, valid_hbm, src_ref, obs_ref, table_ref, after_ref, design, piece_ref, acc, slot_ref, valid_ref, sems
):
    del after_ref
    copies = begin_copies(((slot_hbm, slot_ref), (valid_hbm, valid_ref)), sems)
    tiles = obs_ref.shape[0]
    owners = table_ref.shape[0]
    acc[...] = jnp.zeros_like(acc)
    lane = iota((PARAMS, LANES), 1)
    zero = jnp.zeros((8, LANES), F32)
    for copy in copies:
        copy.wait()

    def body(step, carry):
        for k in range(UNROLL):
            t = step * UNROLL + k
            rows = jnp.where(lane < valid_ref[t], src_ref[pl.ds(t, PARAMS, stride=tiles), :], 0.0)
            design[t] = zero
            design[t, 0:PARAMS, :] = rows
            acc[slot_ref[t], 0:PARAMS, :] += rows * row_of(obs_ref, t)[0:PARAMS]
        return carry

    lax.fori_loop(0, tiles // UNROLL, body, 0)
    col = iota((CAP, LANES), 1)
    placed = (col % CAP == iota((CAP, LANES), 0)).astype(BF16)
    names = jnp.dot(table_ref[...].astype(F32).astype(BF16), placed, preferred_element_type=F32)
    col = iota((owners, LANES), 1)
    owner = iota((owners, LANES), 0)
    names = jnp.where(col // CAP == owner, names + (owner * SB_DEV).astype(F32), 0.0)
    names = jnp.sum(names, axis=0, keepdims=True)
    names = jnp.where(iota((8, LANES), 0) == 0, jnp.broadcast_to(names, (8, LANES)), 0.0)
    send_slots(acc, piece_ref, names)


def later_sources(slot_hbm, design, y_ref, numbers_ref, piece_ref, acc, slot_ref, sems):
    [copy] = begin_copies(((slot_hbm, slot_ref),), sems)
    tiles = y_ref.shape[0]
    acc[...] = jnp.zeros_like(acc)

    copy.wait()

    def body(step, carry):
        for k in range(UNROLL):
            t = step * UNROLL + k
            acc[slot_ref[t]] += design[t] * row_of(y_ref, t)
        return carry

    lax.fori_loop(0, tiles // UNROLL, body, 0)
    send_slots(acc, piece_ref, numbers_ref[...])


def att_kernel(*refs):
    level, out_ref = [part[...] for part in refs[:-1]], refs[-1]
    while len(level) > 1:
        level = [level[k] + level[k + 1] for k in range(0, len(level), 2)]
    out_ref[...] = level[0]


def rim_kernel(part_ref, near_ref, far_ref, out_ref):
    owners = lax.axis_size("tm")
    me = lax.axis_index("tm")
    even = jnp.full((8, LANES), me % 2, jnp.int32) == 0
    near, far = near_ref[...], far_ref[...]
    left = jnp.where(me > 0, jnp.where(even, far, near), 0.0)
    right = jnp.where(me < owners - 1, jnp.where(even, near, far), 0.0)
    has_right = jnp.where(me < owners - 1, 1.0, 0.0)
    out_ref[...] = part_ref[...]
    for axis in range(AXES):
        at = axis * ROWS_PAD
        out_ref[at : at + 1, :] = part_ref[at : at + 1, :] + left[4 + axis : 5 + axis]
        at = at + ROWS
        out_ref[at : at + 1, :] = has_right * part_ref[at : at + 1, :] + right[axis : axis + 1]


def dense_kernel(slots, with_names, *refs):
    if with_names:
        refs, names_out = refs[:-1], refs[-1]
    else:
        names_in, refs = refs[0], refs[1:]
    pieces, dense_ref = refs[:-2], refs[-1]
    blocks = (dense_ref.shape[0] - 8) // PARAMS
    last = PARAMS * slots
    extras = [piece[last : last + 8, :] for piece in pieces]
    if with_names:
        names = [extra[0:1] for extra in extras]
        out = jnp.zeros(names_out.shape, F32)
        for k, name in enumerate(names):
            out = jnp.where(iota(out.shape, 0) == k, jnp.broadcast_to(name, out.shape), out)
        names_out[...] = out
    else:
        names = [names_in[k : k + 1, :] for k in range(len(pieces))]
    block = iota((blocks, slots), 0).astype(F32)
    hot = jnp.concatenate(
        [
            jnp.where(block == jnp.broadcast_to(name[:, 0:slots], block.shape), 1.0, 0.0).astype(BF16)
            for name in names
        ],
        axis=1,
    )
    got = jnp.concatenate(
        [
            jnp.concatenate([piece[p * slots : p * slots + slots, :] for piece in pieces], axis=0)
            for p in range(PARAMS)
        ],
        axis=1,
    )
    three = [jnp.dot(hot, part, preferred_element_type=F32) for part in split3(got)]
    summed = (three[2] + three[1]) + three[0]
    for param in range(PARAMS):
        dense_ref[param * blocks : param * blocks + blocks, :] = summed[:, param * LANES : (param + 1) * LANES]
    numbers = extras[0]
    for extra in extras[1:]:
        numbers = numbers + extra
    dense_ref[PARAMS * blocks :, :] = numbers


def load_vector(mine_ref, other_ref, parts, dense, table, true_ref, own_ref):
    rows = mine_ref.shape[0] - 8
    blocks = rows // PARAMS
    me = lax.axis_index("tm")
    dense[0:rows, :] = mine_ref[0:rows, :] + other_ref[0:rows, :]
    dense[rows:, :] = jnp.zeros((dense.shape[0] - rows, LANES), F32)
    for param in range(PARAMS):
        at = pl.multiple_of(param * blocks + me * SB_DEV, SB_DEV)
        own_ref[param] = dense[pl.ds(at, SB_DEV), :]
    sub = iota((8, LANES), 0)
    lane = iota((8, LANES), 1)
    low = sub < 4
    axis_of = sub % 4
    level = [part[...] for part in parts]
    while len(level) > 1:
        level = [level[k] + level[k + 1] for k in range(0, len(level), 2)]
    att = level[0]
    for axis in range(AXES):
        true_ref[axis] = att[axis * ROWS_PAD : axis * ROWS_PAD + ROWS]

    def mixed(row):
        three = [att[axis * ROWS_PAD + row : axis * ROWS_PAD + row + 1] for axis in range(AXES)]
        three = [jnp.broadcast_to(v, (8, LANES)) for v in three]
        out = jnp.where(axis_of == 0, three[0], jnp.where(axis_of == 1, three[1], three[2]))
        return jnp.where(axis_of < 3, out, 0.0)

    def rolled(value):
        return [pltpu.roll(value, LANES - k, 1) for k in (1, 2, 3)]

    now = mixed(0)
    now_rolled = rolled(now)
    for row in range(ROWS + 1):
        after = mixed(row + 1) if row < ROWS else jnp.zeros((8, LANES), F32)
        after_rolled = rolled(after)
        moved = [jnp.where(lane < LANES - 1 - k, now_rolled[k], after_rolled[k]) for k in range(3)]
        table[row, 0:8, :] = jnp.where(low, now, moved[0])
        table[row, 8:16, :] = jnp.where(low, moved[1], moved[2])
        now, now_rolled = after, after_rolled


def forward(tiles, where, design, sources, slot_ref, offset_ref, block_ref, dense, table):
    blocks = dense.shape[0] // 8
    values = []
    for t, (lane, first) in zip(tiles, where):
        row = offset_ref[t] // LANES
        slot = slot_ref[t]
        block = slot // CAP * SB_DEV + block_ref[slot // CAP, slot % CAP]
        summed = sources[t] * dense[pl.ds(block, 8, stride=blocks), :]
        for half in (0, 8):
            here = jnp.take_along_axis(table[row, half : half + 8, :], lane, axis=1)
            there = jnp.take_along_axis(table[row + 1, half : half + 8, :], lane, axis=1)
            summed = summed + design[t, half : half + 8, :] * jnp.where(first, here, there)
        summed = summed + pltpu.roll(summed, 4, 0)
        summed = summed + pltpu.roll(summed, 2, 0)
        values.append(summed + pltpu.roll(summed, 1, 0))
    return values


def middle_kernel(
    copies,
    slot_hbm,
    offset_hbm,
    block_hbm,
    mine_ref,
    other_ref,
    design,
    sources,
    knot_ref,
    *refs,
):
    parts = refs[:1]
    numbers_ref, sum_ref, rim_ref, true_ref, own_ref, y_ref, knots, dense, table, slot_ref, offset_ref, block_ref, sems = refs[1:]
    copies_in = begin_copies(
        ((slot_hbm, slot_ref), (offset_hbm, offset_ref), (block_hbm, block_ref)), sems
    )
    tiles = design.shape[0]
    knots[...] = jnp.zeros_like(knots)
    sum_ref[...] = jnp.zeros_like(sum_ref)
    load_vector(mine_ref, other_ref, parts, dense, table, true_ref, own_ref)

    for copy in copies_in:
        copy.wait()

    def body(step, carry):
        batch = [step * UNROLL + k for k in range(UNROLL)]
        where = [places(t, offset_ref, knot_ref) for t in batch]
        values = forward(batch, where, design, sources, slot_ref, offset_ref, block_ref, dense, table)
        for t, value in zip(batch, values):
            y_ref[pl.ds(t, 1), :] = value[0:1]
        add_adjoint(batch, values, where, design, offset_ref, knots)
        return carry

    lax.fori_loop(0, tiles // UNROLL, body, 0)
    square = y_ref[...] * y_ref[...]
    send_sums(knots, sum_ref, rim_ref)
    norm_att = true_ref[0] * true_ref[0]
    for axis in range(1, AXES):
        norm_att = norm_att + true_ref[axis] * true_ref[axis]
    norm_src = own_ref[0] * own_ref[0]
    for param in range(1, PARAMS):
        norm_src = norm_src + own_ref[param] * own_ref[param]
    norm = total(norm_src) + total(norm_att) / copies
    lane = iota((8, LANES), 1)
    numbers = jnp.where(lane == 0, total(square), jnp.where(lane == 1, norm, 0.0))
    numbers_ref[...] = jnp.where(iota((8, LANES), 0) == 1, numbers, 0.0)


def last_kernel(
    copies,
    slot_hbm,
    offset_hbm,
    block_hbm,
    mine_ref,
    other_ref,
    design,
    sources,
    knot_ref,
    y_ref,
    numbers_ref,
    z_att,
    z_src,
    *refs,
):
    parts = refs[:1]
    true_ref, own_ref, out_ref, dense, table, after_ref, slot_ref, offset_ref, block_ref, sems = refs[1:]
    copies_in = begin_copies(
        ((slot_hbm, slot_ref), (offset_hbm, offset_ref), (block_hbm, block_ref)), sems
    )
    tiles = design.shape[0]
    rows = mine_ref.shape[0] - 8
    owners = rows // (PARAMS * SB_DEV)
    load_vector(mine_ref, other_ref, parts, dense, table, true_ref, own_ref)
    group = (mine_ref[rows:, :] + other_ref[rows:, :])[1:2]
    s_group, n_group = group[:, 0:1], group[:, 1:2]
    sigma = s_group / n_group

    def about(new, old, count):
        square, across = None, None
        for k in range(count):
            rest = new[k] - sigma * old[k]
            first, second = rest * rest, rest * old[k]
            square = first if square is None else square + first
            across = second if across is None else across + second
        return total(square), total(across)

    att, src = about(true_ref, z_att, AXES), about(own_ref, z_src, PARAMS)
    d_square = src[0] + att[0] / copies
    d_across = src[1] + att[1] / copies
    tau = sigma + owners * d_square / (s_group + n_group)

    for copy in copies_in:
        copy.wait()

    def body(step, carry):
        batch = [step * UNROLL + k for k in range(UNROLL)]
        where = [places(t, offset_ref, knot_ref) for t in batch]
        values = forward(batch, where, design, sources, slot_ref, offset_ref, block_ref, dense, table)
        for t, value in zip(batch, values):
            after_ref[pl.ds(t, 1), :] = value[0:1]
        return carry

    lax.fori_loop(0, tiles // UNROLL, body, 0)
    rest = after_ref[...] - tau * y_ref[...]
    square, across = rest * rest, rest * y_ref[...]
    own = numbers_ref[1:2, :]
    numbers = [
        own[:, 1:2],
        own[:, 0:1],
        d_square,
        d_across,
        sigma,
        total(square),
        total(across),
        tau,
    ]
    lane = iota((1, LANES), 1)
    out = jnp.zeros((1, LANES), F32)
    for k, number in enumerate(numbers):
        out = jnp.where(lane == k, number, out)
    out_ref[...] = jnp.broadcast_to(out[None], out_ref.shape)


def final_kernel(got_ref, z_src, w_src, z_att, w_att, src_out, att_out):
    devices = got_ref.shape[0]
    got = got_ref[...].reshape(devices, LANES)

    def column(k):
        return got[:, k : k + 1]

    def summed(value):
        return jnp.sum(value, axis=0, keepdims=True)

    n_of, s_of = column(0), column(1)
    n, s = summed(n_of), summed(s_of)
    sigma = s / n
    alpha = n / (s + n)
    off = column(4) - sigma
    d = summed(column(2) + 2.0 * off * column(3) + off * off * n_of)
    gamma = alpha * d / n
    tau = sigma + gamma
    off = column(7) - tau
    e = summed(column(5) + 2.0 * off * column(6) + off * off * s_of)
    second = d / (e + damping * (d + gamma * gamma * n))
    c_z = alpha * (1.0 + second * tau)
    c_w = alpha * second
    for param in range(PARAMS):
        src_out[param] = c_z * z_src[param] - c_w * w_src[param]
    for axis in range(AXES):
        value = c_z * z_att[axis] - c_w * w_att[axis]
        for row in range(ROWS):
            att_out[axis : axis + 1, row * LANES : (row + 1) * LANES] = value[row : row + 1]


VMEM = pl.BlockSpec(memory_space=pltpu.VMEM)
ANY = pl.BlockSpec(memory_space=pl.ANY)
SMEM = pl.BlockSpec(memory_space=pltpu.SMEM)
HBM = pl.BlockSpec(memory_space=pltpu.HBM)
MIB = 1024 * 1024


HIDES = pl.CostEstimate(flops=3 * 10**10, bytes_accessed=0, transcendentals=0)


def f32(*shape):
    return jax.ShapeDtypeStruct(shape, F32)


def call(kernel, out_shape, in_specs, scratch=(), name=None, grant=16, cost=None):
    return pl.pallas_call(
        kernel,
        out_shape=out_shape,
        in_specs=in_specs,
        out_specs=jax.tree.map(lambda _: VMEM, out_shape),
        scratch_shapes=list(scratch),
        compiler_params=pltpu.CompilerParams(vmem_limit_bytes=grant * MIB),
        cost_estimate=cost,
        name=name,
    )


def shards(
    src_design,
    att_design,
    obs_frac,
    obs_knot,
    observed,
    tile_slot,
    tile_offset,
    tile_valid,
    slot_block,
):
    tiles = src_design.shape[0]
    owners = lax.axis_size("tm")
    copies = lax.axis_size("src")
    devices = owners * copies
    slots = owners * CAP
    blocks = owners * SB_DEV
    acc = pltpu.VMEM((slots, 8, LANES), F32)
    knots = pltpu.VMEM((ROWS + 1, 16, LANES), F32)
    dense = pltpu.VMEM((8 * blocks, LANES), F32)
    piece = f32(PARAMS * slots + 8, LANES)
    summed = f32(PARAMS * blocks + 8, LANES)
    part = f32(AXES * ROWS_PAD, LANES)
    true = f32(AXES, ROWS, LANES)
    mine = f32(PARAMS, SB_DEV, LANES)
    rim = f32(8, LANES)

    def flipped(value, axis, bits):
        size = lax.axis_size(axis)
        return lax.ppermute(value, axis, [(i, i ^ bits) for i in range(size)])

    def att_sums(own, rims):
        near = flipped(rims, "tm", 1)
        route = [(i, i + 1) for i in range(1, owners - 1, 2)]
        far = lax.ppermute(rims, "tm", route + [(j, i) for i, j in route])
        own = call(rim_kernel, part, [VMEM] * 3, name="rims")(own, near, far)
        parts = [own] + [flipped(own, "src", k) for k in range(1, copies)]
        return own, call(att_kernel, part, [VMEM] * copies, name="att", cost=HIDES)(*parts)

    def src_sums(pieces, names, after):
        sent = [pieces] + [flipped(pieces, "tm", k) for k in range(2, owners, 2)]
        count = owners // 2
        if names is None:
            half, names = call(
                functools.partial(dense_kernel, slots, True),
                (summed, f32((count + 7) // 8 * 8, LANES)),
                [VMEM] * count + [ANY],
                name="dense_first",
            )(*sent, after)
        else:
            half = call(
                functools.partial(dense_kernel, slots, False),
                summed,
                [VMEM] * (1 + count) + [ANY],
                name="dense_second",
            )(names, *sent, after)
        return half, flipped(half, "tm", 1), names

    def held(value):
        return pltpu.with_memory_space_constraint(value, pltpu.HBM)

    src_rows = jnp.transpose(src_design, (1, 0, 2)).reshape(PARAMS * tiles, LANES)
    att_rows = jnp.transpose(att_design, (1, 0, 2)).reshape(AXES * tiles, LANES)
    whole = (tiles, LANES)
    design, own, rims = call(
        first_kernel,
        (f32(tiles, 16, LANES), part, rim),
        [HBM] * 6,
        [
            knots,
            pltpu.VMEM((4, tiles, LANES), F32),
            pltpu.SMEM((tiles,), jnp.int32),
            pltpu.SMEM((tiles,), jnp.int32),
            pltpu.VMEM((AXES * tiles, LANES), F32),
            pltpu.VMEM(whole, F32),
            pltpu.VMEM(whole, jnp.int32),
            pltpu.VMEM(whole, F32),
            pltpu.SemaphoreType.DMA((6,)),
        ],
        "first",
    )(*[
        pltpu.with_memory_space_constraint(value, pltpu.HBM)
        for value in (tile_offset, tile_valid, att_rows, obs_frac, obs_knot, observed)
    ])
    sources, pieces = call(
        first_sources,
        (f32(tiles, 8, LANES), piece),
        [HBM] * 2 + [VMEM] * 3 + [ANY],
        [acc] + [pltpu.SMEM((tiles,), jnp.int32)] * 2 + [pltpu.SemaphoreType.DMA((2,))],
        "first_sources",
    )(held(tile_slot), held(tile_valid), src_rows, observed, slot_block, own)
    own, att = att_sums(own, rims)
    half, other, names = src_sums(pieces, None, own)
    numbers, own, rims, z_att, z_src, y = call(
        functools.partial(middle_kernel, copies),
        (rim, part, rim, true, mine, f32(tiles, LANES)),
        [HBM] * 3 + [VMEM] * 6,
        [knots, dense, knots]
        + [pltpu.SMEM((tiles,), jnp.int32)] * 2
        + [pltpu.SMEM(slot_block.shape, jnp.int32), pltpu.SemaphoreType.DMA((3,))],
        "middle",
    )(held(tile_slot), held(tile_offset), held(slot_block), half, other, design, sources, obs_knot, att)
    pieces = call(
        later_sources,
        piece,
        [HBM] + [VMEM] * 3,
        [acc, pltpu.SMEM((tiles,), jnp.int32), pltpu.SemaphoreType.DMA((1,))],
        "later_sources",
    )(held(tile_slot), sources, y, numbers)
    own, att = att_sums(own, rims)
    half, other, names = src_sums(pieces, names, own)
    w_att, w_src, row = call(
        functools.partial(last_kernel, copies),
        (true, mine, f32(devices, 1, LANES)),
        [HBM] * 3 + [VMEM] * 10,
        [dense, knots, pltpu.VMEM((tiles, LANES), F32)]
        + [pltpu.SMEM((tiles,), jnp.int32)] * 2
        + [pltpu.SMEM(slot_block.shape, jnp.int32), pltpu.SemaphoreType.DMA((3,))],
        "last",
    )(
        held(tile_slot), held(tile_offset), held(slot_block), half, other, design, sources, obs_knot, y, numbers, z_att, z_src, att
    )
    row = lax.all_to_all(row, ("src", "tm"), 0, 0, tiled=True)
    src, att = call(
        final_kernel,
        (mine, f32(AXES, KN)),
        [VMEM] * 5,
        name="final",
    )(row, z_src, w_src, z_att, w_att)
    return jnp.transpose(src, (1, 0, 2)), att


def solution(mesh):
    placed = (
        P(("src", "tm"), None, None),
        P(("src", "tm"), None, None),
        P(("src", "tm"), None),
        P(("src", "tm"), None),
        P(("src", "tm"), None),
        P(("src", "tm")),
        P(("src", "tm")),
        P(("src", "tm")),
        P(("src", "tm"), None),
    )
    return jax.shard_map(
        shards,
        mesh=mesh,
        in_specs=placed,
        out_specs=(P(("src", "tm"), None, None), P(None, "tm")),
        check_vma=False,
    )
```

```python
import functools

import jax
import jax.numpy as jnp
from jax import lax
from jax.experimental import pallas as pl
from jax.experimental.pallas import tpu as pltpu
from jax.sharding import PartitionSpec as P

KN = 4096
HW = 128
SB_DEV = 32
damping = 1.0

LANES = 128
ROWS = KN // LANES
AXES = 3
PART = AXES * ROWS + 8
PARAMS = 5
CAP = 8
UNROLL = 128
F32 = jnp.float32
BF16 = jnp.bfloat16


def place_of(axis, row):
    return axis * ROWS + row if row < ROWS else AXES * ROWS + axis


def iota(shape, dim):
    return lax.broadcasted_iota(jnp.int32, shape, dim)


def spline_weights(fraction):
    remain = 1.0 - fraction
    square = fraction * fraction
    cubed = square * fraction
    return (
        remain * remain * remain / 6.0,
        (3.0 * cubed - 6.0 * square + 4.0) / 6.0,
        (-3.0 * cubed + 3.0 * square + 3.0 * fraction + 1.0) / 6.0,
        cubed / 6.0,
    )


def split2(value):
    high = value.astype(BF16)
    return high, (value - high.astype(F32)).astype(BF16)


def split3(value):
    high, rest = value.astype(BF16), None
    rest = value - high.astype(F32)
    middle = rest.astype(BF16)
    return high, middle, (rest - middle.astype(F32)).astype(BF16)


def total(value):
    return jnp.sum(jnp.sum(value, axis=0, keepdims=True), axis=1, keepdims=True)


def row_of(ref, row):
    return jnp.broadcast_to(ref[pl.ds(row, 1), :], (8, LANES))


def places(t, offset_ref, knot_ref):
    place = row_of(knot_ref, t) + offset_ref[t] % LANES
    first = place < LANES
    return jnp.where(first, place, place - LANES), first


def add_adjoint(tiles, values, where, design, offset_ref, knots):
    lane_row = iota((LANES, LANES), 0).astype(F32).astype(BF16)
    yes, no = jnp.ones((), BF16), jnp.zeros((), BF16)
    outs = []
    for t, resid, (lane, first) in zip(tiles, values, where):
        lane, first = lane[0:1], first[0:1]
        hot = jnp.where(lane_row == lane.astype(F32).astype(BF16), yes, no)
        high, low = split2(
            jnp.concatenate([design[t, 0:8, :] * resid, design[t, 8:16, :] * resid], axis=0)
        )
        here = jnp.broadcast_to(jnp.where(first, 1.0, 0.0).astype(BF16), high.shape)
        parts = (high * here, low * here)
        parts = parts + (high - parts[0], low - parts[1])
        outs.append(
            lax.dot_general(
                jnp.concatenate(parts, axis=0),
                hot,
                (((1,), (1,)), ((), ())),
                preferred_element_type=F32,
            )
        )
    for t, out in zip(tiles, outs):
        row = offset_ref[t] // LANES
        knots[row] += out[0:16] + out[16:32]
        knots[row + 1] += out[32:48] + out[48:64]


def send_sums(knots, att_ref, rim_ref):
    lane = iota((8, LANES), 1)
    low = iota((8, LANES), 0) < 4
    before = [jnp.zeros((8, LANES), F32)] * 3
    for row in range(ROWS + 1):
        one, two = knots[row, 0:8, :], knots[row, 8:16, :]
        now = [pltpu.roll(one, 1, 1), pltpu.roll(two, 2, 1), pltpu.roll(two, 3, 1)]
        moved = [jnp.where(lane >= k + 1, now[k], before[k]) for k in range(3)]
        both = jnp.where(low, one + moved[1], moved[0] + moved[2])
        both = both + pltpu.roll(both, 4, 0)
        for axis in range(AXES):
            at = place_of(axis, row)
            att_ref[at : at + 1, :] = both[axis : axis + 1]
        if row == 0:
            rim_ref[...] = both
        before = now
    moved = pltpu.roll(both, 4, 0)
    rim_ref[...] = jnp.where(low, rim_ref[...], moved)


def first_kernel(
    offset_hbm,
    valid_hbm,
    att_hbm,
    frac_hbm,
    knot_hbm,
    obs_hbm,
    design,
    part_ref,
    rim_ref,
    knots,
    wts,
    offset_ref,
    valid_ref,
    att_ref,
    frac_ref,
    knot_ref,
    obs_ref,
    sems,
):
    pairs = (
        (frac_hbm, frac_ref),
        (offset_hbm, offset_ref),
        (valid_hbm, valid_ref),
        (knot_hbm, knot_ref),
        (obs_hbm, obs_ref),
        (att_hbm, att_ref),
    )
    copies = [pltpu.make_async_copy(a, b, sems.at[k]) for k, (a, b) in enumerate(pairs)]
    for copy in copies:
        copy.start()
    tiles = knot_ref.shape[0]
    knots[...] = jnp.zeros_like(knots)
    part_ref[...] = jnp.zeros_like(part_ref)
    for copy in copies:
        copy.wait()
    for k, weight in enumerate(spline_weights(frac_ref[...])):
        wts[k] = weight
    sub = iota((8, LANES), 0)
    lane = iota((8, LANES), 1)
    axis_of = sub % 4

    def body(step, carry):
        batch = [step * UNROLL + k for k in range(UNROLL)]
        for t in batch:
            live = lane < valid_ref[t]
            three = [row_of(att_ref, axis * tiles + t) for axis in range(AXES)]
            mixed = jnp.where(axis_of == 0, three[0], jnp.where(axis_of == 1, three[1], three[2]))
            mixed = jnp.where(live & (axis_of < 3), mixed, 0.0)
            weights = [row_of(wts.at[k], t) for k in range(4)]
            design[t, 0:8, :] = mixed * jnp.where(sub < 4, weights[0], weights[1])
            design[t, 8:16, :] = mixed * jnp.where(sub < 4, weights[2], weights[3])
        values = [row_of(obs_ref, t) for t in batch]
        where = [places(t, offset_ref, knot_ref) for t in batch]
        add_adjoint(batch, values, where, design, offset_ref, knots)
        return carry

    lax.fori_loop(0, tiles // UNROLL, body, 0)
    send_sums(knots, part_ref, rim_ref)


def begin_copies(pairs, sems):
    copies = [pltpu.make_async_copy(a, b, sems.at[k]) for k, (a, b) in enumerate(pairs)]
    for copy in copies:
        copy.start()
    return copies


def send_slots(acc, piece_ref, extra):
    slots = acc.shape[0]
    for param in range(PARAMS):
        for at in range(0, slots, 8):
            piece_ref[param * slots + at : param * slots + at + 8, :] = acc[at : at + 8, param, :]
    piece_ref[PARAMS * slots :, :] = extra


def first_sources(
    slot_hbm, valid_hbm, src_ref, obs_ref, table_ref, after_ref, design, piece_ref, acc, slot_ref, valid_ref, sems
):
    del after_ref
    copies = begin_copies(((slot_hbm, slot_ref), (valid_hbm, valid_ref)), sems)
    tiles = obs_ref.shape[0]
    owners = table_ref.shape[0]
    acc[...] = jnp.zeros_like(acc)
    lane = iota((PARAMS, LANES), 1)
    zero = jnp.zeros((8, LANES), F32)
    for copy in copies:
        copy.wait()

    def body(step, carry):
        for k in range(UNROLL):
            t = step * UNROLL + k
            rows = jnp.where(lane < valid_ref[t], src_ref[pl.ds(t, PARAMS, stride=tiles), :], 0.0)
            design[t] = zero
            design[t, 0:PARAMS, :] = rows
            acc[slot_ref[t], 0:PARAMS, :] += rows * row_of(obs_ref, t)[0:PARAMS]
        return carry

    lax.fori_loop(0, tiles // UNROLL, body, 0)
    col = iota((CAP, LANES), 1)
    placed = (col % CAP == iota((CAP, LANES), 0)).astype(BF16)
    names = jnp.dot(table_ref[...].astype(F32).astype(BF16), placed, preferred_element_type=F32)
    col = iota((owners, LANES), 1)
    owner = iota((owners, LANES), 0)
    names = jnp.where(col // CAP == owner, names + (owner * SB_DEV).astype(F32), 0.0)
    names = jnp.sum(names, axis=0, keepdims=True)
    names = jnp.where(iota((8, LANES), 0) == 0, jnp.broadcast_to(names, (8, LANES)), 0.0)
    send_slots(acc, piece_ref, names)


def later_sources(slot_hbm, design, y_ref, numbers_ref, piece_ref, acc, slot_ref, sems):
    [copy] = begin_copies(((slot_hbm, slot_ref),), sems)
    tiles = y_ref.shape[0]
    acc[...] = jnp.zeros_like(acc)

    copy.wait()

    def body(step, carry):
        for k in range(UNROLL):
            t = step * UNROLL + k
            acc[slot_ref[t]] += design[t] * row_of(y_ref, t)
        return carry

    lax.fori_loop(0, tiles // UNROLL, body, 0)
    send_slots(acc, piece_ref, numbers_ref[...])


def att_kernel(*refs):
    level, out_ref = [part[...] for part in refs[:-1]], refs[-1]
    while len(level) > 1:
        level = [level[k] + level[k + 1] for k in range(0, len(level), 2)]
    out_ref[...] = level[0]


def rim_kernel(part_ref, near_ref, far_ref, out_ref):
    owners = lax.axis_size("tm")
    me = lax.axis_index("tm")
    even = jnp.full((8, LANES), me % 2, jnp.int32) == 0
    near, far = near_ref[...], far_ref[...]
    left = jnp.where(me > 0, jnp.where(even, far, near), 0.0)
    right = jnp.where(me < owners - 1, jnp.where(even, near, far), 0.0)
    has_right = jnp.where(me < owners - 1, 1.0, 0.0)
    out_ref[...] = part_ref[...]
    for axis in range(AXES):
        at = place_of(axis, 0)
        out_ref[at : at + 1, :] = part_ref[at : at + 1, :] + left[4 + axis : 5 + axis]
        at = place_of(axis, ROWS)
        out_ref[at : at + 1, :] = has_right * part_ref[at : at + 1, :] + right[axis : axis + 1]


def dense_kernel(slots, with_names, *refs):
    if with_names:
        refs, names_out = refs[:-1], refs[-1]
    else:
        names_in, refs = refs[0], refs[1:]
    pieces, dense_ref = refs[:-2], refs[-1]
    blocks = (dense_ref.shape[0] - 8) // PARAMS
    last = PARAMS * slots
    extras = [piece[last : last + 8, :] for piece in pieces]
    if with_names:
        names = [extra[0:1] for extra in extras]
        out = jnp.zeros(names_out.shape, F32)
        for k, name in enumerate(names):
            out = jnp.where(iota(out.shape, 0) == k, jnp.broadcast_to(name, out.shape), out)
        names_out[...] = out
    else:
        names = [names_in[k : k + 1, :] for k in range(len(pieces))]
    block = iota((blocks, slots), 0).astype(F32)
    hot = jnp.concatenate(
        [
            jnp.where(block == jnp.broadcast_to(name[:, 0:slots], block.shape), 1.0, 0.0).astype(BF16)
            for name in names
        ],
        axis=1,
    )
    got = jnp.concatenate(
        [
            jnp.concatenate([piece[p * slots : p * slots + slots, :] for piece in pieces], axis=0)
            for p in range(PARAMS)
        ],
        axis=1,
    )
    three = [jnp.dot(hot, part, preferred_element_type=F32) for part in split3(got)]
    summed = (three[2] + three[1]) + three[0]
    for param in range(PARAMS):
        dense_ref[param * blocks : param * blocks + blocks, :] = summed[:, param * LANES : (param + 1) * LANES]
    numbers = extras[0]
    for extra in extras[1:]:
        numbers = numbers + extra
    dense_ref[PARAMS * blocks :, :] = numbers


def load_vector(mine_ref, other_ref, parts, dense, table, true_ref, own_ref):
    rows = mine_ref.shape[0] - 8
    blocks = rows // PARAMS
    me = lax.axis_index("tm")
    dense[0:rows, :] = mine_ref[0:rows, :] + other_ref[0:rows, :]
    dense[rows:, :] = jnp.zeros((dense.shape[0] - rows, LANES), F32)
    for param in range(PARAMS):
        at = pl.multiple_of(param * blocks + me * SB_DEV, SB_DEV)
        own_ref[param] = dense[pl.ds(at, SB_DEV), :]
    sub = iota((8, LANES), 0)
    lane = iota((8, LANES), 1)
    low = sub < 4
    axis_of = sub % 4
    level = [part[...] for part in parts]
    while len(level) > 1:
        level = [level[k] + level[k + 1] for k in range(0, len(level), 2)]
    att = level[0]
    for axis in range(AXES):
        true_ref[axis] = att[axis * ROWS : axis * ROWS + ROWS]

    def mixed(row):
        three = [att[place_of(axis, row) : place_of(axis, row) + 1] for axis in range(AXES)]
        three = [jnp.broadcast_to(v, (8, LANES)) for v in three]
        out = jnp.where(axis_of == 0, three[0], jnp.where(axis_of == 1, three[1], three[2]))
        return jnp.where(axis_of < 3, out, 0.0)

    def rolled(value):
        return [pltpu.roll(value, LANES - k, 1) for k in (1, 2, 3)]

    now = mixed(0)
    now_rolled = rolled(now)
    for row in range(ROWS + 1):
        after = mixed(row + 1) if row < ROWS else jnp.zeros((8, LANES), F32)
        after_rolled = rolled(after)
        moved = [jnp.where(lane < LANES - 1 - k, now_rolled[k], after_rolled[k]) for k in range(3)]
        table[row, 0:8, :] = jnp.where(low, now, moved[0])
        table[row, 8:16, :] = jnp.where(low, moved[1], moved[2])
        now, now_rolled = after, after_rolled


def forward(tiles, where, design, sources, slot_ref, offset_ref, block_ref, dense, table):
    blocks = dense.shape[0] // 8
    values = []
    for t, (lane, first) in zip(tiles, where):
        row = offset_ref[t] // LANES
        slot = slot_ref[t]
        block = slot // CAP * SB_DEV + block_ref[slot // CAP, slot % CAP]
        summed = sources[t] * dense[pl.ds(block, 8, stride=blocks), :]
        for half in (0, 8):
            here = jnp.take_along_axis(table[row, half : half + 8, :], lane, axis=1)
            there = jnp.take_along_axis(table[row + 1, half : half + 8, :], lane, axis=1)
            summed = summed + design[t, half : half + 8, :] * jnp.where(first, here, there)
        summed = summed + pltpu.roll(summed, 4, 0)
        summed = summed + pltpu.roll(summed, 2, 0)
        values.append(summed + pltpu.roll(summed, 1, 0))
    return values


def middle_kernel(
    copies,
    slot_hbm,
    offset_hbm,
    block_hbm,
    mine_ref,
    other_ref,
    design,
    sources,
    knot_ref,
    *refs,
):
    parts = refs[:1]
    numbers_ref, sum_ref, rim_ref, true_ref, own_ref, y_ref, knots, dense, table, slot_ref, offset_ref, block_ref, sems = refs[1:]
    copies_in = begin_copies(
        ((slot_hbm, slot_ref), (offset_hbm, offset_ref), (block_hbm, block_ref)), sems
    )
    tiles = design.shape[0]
    knots[...] = jnp.zeros_like(knots)
    sum_ref[...] = jnp.zeros_like(sum_ref)
    load_vector(mine_ref, other_ref, parts, dense, table, true_ref, own_ref)

    for copy in copies_in:
        copy.wait()

    def body(step, carry):
        batch = [step * UNROLL + k for k in range(UNROLL)]
        where = [places(t, offset_ref, knot_ref) for t in batch]
        values = forward(batch, where, design, sources, slot_ref, offset_ref, block_ref, dense, table)
        for t, value in zip(batch, values):
            y_ref[pl.ds(t, 1), :] = value[0:1]
        add_adjoint(batch, values, where, design, offset_ref, knots)
        return carry

    lax.fori_loop(0, tiles // UNROLL, body, 0)
    square = y_ref[...] * y_ref[...]
    send_sums(knots, sum_ref, rim_ref)
    norm_att = true_ref[0] * true_ref[0]
    for axis in range(1, AXES):
        norm_att = norm_att + true_ref[axis] * true_ref[axis]
    norm_src = own_ref[0] * own_ref[0]
    for param in range(1, PARAMS):
        norm_src = norm_src + own_ref[param] * own_ref[param]
    norm = total(norm_src) + total(norm_att) / copies
    lane = iota((8, LANES), 1)
    numbers = jnp.where(lane == 0, total(square), jnp.where(lane == 1, norm, 0.0))
    numbers_ref[...] = jnp.where(iota((8, LANES), 0) == 1, numbers, 0.0)


def last_kernel(
    copies,
    slot_hbm,
    offset_hbm,
    block_hbm,
    mine_ref,
    other_ref,
    design,
    sources,
    knot_ref,
    y_ref,
    numbers_ref,
    z_att,
    z_src,
    *refs,
):
    parts = refs[:1]
    true_ref, own_ref, out_ref, dense, table, after_ref, slot_ref, offset_ref, block_ref, sems = refs[1:]
    copies_in = begin_copies(
        ((slot_hbm, slot_ref), (offset_hbm, offset_ref), (block_hbm, block_ref)), sems
    )
    tiles = design.shape[0]
    rows = mine_ref.shape[0] - 8
    owners = rows // (PARAMS * SB_DEV)
    load_vector(mine_ref, other_ref, parts, dense, table, true_ref, own_ref)
    group = (mine_ref[rows:, :] + other_ref[rows:, :])[1:2]
    s_group, n_group = group[:, 0:1], group[:, 1:2]
    sigma = s_group / n_group

    def about(new, old, count):
        square, across = None, None
        for k in range(count):
            rest = new[k] - sigma * old[k]
            first, second = rest * rest, rest * old[k]
            square = first if square is None else square + first
            across = second if across is None else across + second
        return total(square), total(across)

    att, src = about(true_ref, z_att, AXES), about(own_ref, z_src, PARAMS)
    d_square = src[0] + att[0] / copies
    d_across = src[1] + att[1] / copies
    tau = sigma + owners * d_square / (s_group + n_group)

    for copy in copies_in:
        copy.wait()

    def body(step, carry):
        batch = [step * UNROLL + k for k in range(UNROLL)]
        where = [places(t, offset_ref, knot_ref) for t in batch]
        values = forward(batch, where, design, sources, slot_ref, offset_ref, block_ref, dense, table)
        for t, value in zip(batch, values):
            after_ref[pl.ds(t, 1), :] = value[0:1]
        return carry

    lax.fori_loop(0, tiles // UNROLL, body, 0)
    rest = after_ref[...] - tau * y_ref[...]
    square, across = rest * rest, rest * y_ref[...]
    own = numbers_ref[1:2, :]
    numbers = [
        own[:, 1:2],
        own[:, 0:1],
        d_square,
        d_across,
        sigma,
        total(square),
        total(across),
        tau,
    ]
    lane = iota((1, LANES), 1)
    out = jnp.zeros((1, LANES), F32)
    for k, number in enumerate(numbers):
        out = jnp.where(lane == k, number, out)
    out_ref[...] = jnp.broadcast_to(out[None], out_ref.shape)


def final_kernel(got_ref, z_src, w_src, z_att, w_att, src_out, att_out):
    devices = got_ref.shape[0]
    got = got_ref[...].reshape(devices, LANES)

    def column(k):
        return got[:, k : k + 1]

    def summed(value):
        return jnp.sum(value, axis=0, keepdims=True)

    n_of, s_of = column(0), column(1)
    n, s = summed(n_of), summed(s_of)
    sigma = s / n
    alpha = n / (s + n)
    off = column(4) - sigma
    d = summed(column(2) + 2.0 * off * column(3) + off * off * n_of)
    gamma = alpha * d / n
    tau = sigma + gamma
    off = column(7) - tau
    e = summed(column(5) + 2.0 * off * column(6) + off * off * s_of)
    second = d / (e + damping * (d + gamma * gamma * n))
    c_z = alpha * (1.0 + second * tau)
    c_w = alpha * second
    for param in range(PARAMS):
        src_out[param] = c_z * z_src[param] - c_w * w_src[param]
    for axis in range(AXES):
        value = c_z * z_att[axis] - c_w * w_att[axis]
        for row in range(ROWS):
            att_out[axis : axis + 1, row * LANES : (row + 1) * LANES] = value[row : row + 1]


VMEM = pl.BlockSpec(memory_space=pltpu.VMEM)
ANY = pl.BlockSpec(memory_space=pl.ANY)
SMEM = pl.BlockSpec(memory_space=pltpu.SMEM)
HBM = pl.BlockSpec(memory_space=pltpu.HBM)
MIB = 1024 * 1024


HIDES = pl.CostEstimate(flops=3 * 10**10, bytes_accessed=0, transcendentals=0)


def f32(*shape):
    return jax.ShapeDtypeStruct(shape, F32)


def call(kernel, out_shape, in_specs, scratch=(), name=None, grant=16, cost=None):
    return pl.pallas_call(
        kernel,
        out_shape=out_shape,
        in_specs=in_specs,
        out_specs=jax.tree.map(lambda _: VMEM, out_shape),
        scratch_shapes=list(scratch),
        compiler_params=pltpu.CompilerParams(vmem_limit_bytes=grant * MIB),
        cost_estimate=cost,
        name=name,
    )


def shards(
    src_design,
    att_design,
    obs_frac,
    obs_knot,
    observed,
    tile_slot,
    tile_offset,
    tile_valid,
    slot_block,
):
    tiles = src_design.shape[0]
    owners = lax.axis_size("tm")
    copies = lax.axis_size("src")
    devices = owners * copies
    slots = owners * CAP
    blocks = owners * SB_DEV
    acc = pltpu.VMEM((slots, 8, LANES), F32)
    knots = pltpu.VMEM((ROWS + 1, 16, LANES), F32)
    dense = pltpu.VMEM((8 * blocks, LANES), F32)
    piece = f32(PARAMS * slots + 8, LANES)
    summed = f32(PARAMS * blocks + 8, LANES)
    part = f32(PART, LANES)
    true = f32(AXES, ROWS, LANES)
    mine = f32(PARAMS, SB_DEV, LANES)
    rim = f32(8, LANES)

    def flipped(value, axis, bits):
        size = lax.axis_size(axis)
        return lax.ppermute(value, axis, [(i, i ^ bits) for i in range(size)])

    def att_sums(own, rims):
        near = flipped(rims, "tm", 1)
        route = [(i, i + 1) for i in range(1, owners - 1, 2)]
        far = lax.ppermute(rims, "tm", route + [(j, i) for i, j in route])
        own = call(rim_kernel, part, [VMEM] * 3, name="rims")(own, near, far)
        parts = [own] + [flipped(own, "src", k) for k in range(1, copies)]
        return own, call(att_kernel, part, [VMEM] * copies, name="att", cost=HIDES)(*parts)

    def src_sums(pieces, names, after):
        sent = [pieces] + [flipped(pieces, "tm", k) for k in range(2, owners, 2)]
        count = owners // 2
        if names is None:
            half, names = call(
                functools.partial(dense_kernel, slots, True),
                (summed, f32((count + 7) // 8 * 8, LANES)),
                [VMEM] * count + [ANY],
                name="dense_first",
            )(*sent, after)
        else:
            half = call(
                functools.partial(dense_kernel, slots, False),
                summed,
                [VMEM] * (1 + count) + [ANY],
                name="dense_second",
            )(names, *sent, after)
        return half, flipped(half, "tm", 1), names

    def held(value):
        return pltpu.with_memory_space_constraint(value, pltpu.HBM)

    src_rows = jnp.transpose(src_design, (1, 0, 2)).reshape(PARAMS * tiles, LANES)
    att_rows = jnp.transpose(att_design, (1, 0, 2)).reshape(AXES * tiles, LANES)
    whole = (tiles, LANES)
    design, own, rims = call(
        first_kernel,
        (f32(tiles, 16, LANES), part, rim),
        [HBM] * 6,
        [
            knots,
            pltpu.VMEM((4, tiles, LANES), F32),
            pltpu.SMEM((tiles,), jnp.int32),
            pltpu.SMEM((tiles,), jnp.int32),
            pltpu.VMEM((AXES * tiles, LANES), F32),
            pltpu.VMEM(whole, F32),
            pltpu.VMEM(whole, jnp.int32),
            pltpu.VMEM(whole, F32),
            pltpu.SemaphoreType.DMA((6,)),
        ],
        "first",
    )(*[
        pltpu.with_memory_space_constraint(value, pltpu.HBM)
        for value in (tile_offset, tile_valid, att_rows, obs_frac, obs_knot, observed)
    ])
    sources, pieces = call(
        first_sources,
        (f32(tiles, 8, LANES), piece),
        [HBM] * 2 + [VMEM] * 3 + [ANY],
        [acc] + [pltpu.SMEM((tiles,), jnp.int32)] * 2 + [pltpu.SemaphoreType.DMA((2,))],
        "first_sources",
    )(held(tile_slot), held(tile_valid), src_rows, observed, slot_block, own)
    own, att = att_sums(own, rims)
    half, other, names = src_sums(pieces, None, own)
    numbers, own, rims, z_att, z_src, y = call(
        functools.partial(middle_kernel, copies),
        (rim, part, rim, true, mine, f32(tiles, LANES)),
        [HBM] * 3 + [VMEM] * 6,
        [knots, dense, knots]
        + [pltpu.SMEM((tiles,), jnp.int32)] * 2
        + [pltpu.SMEM(slot_block.shape, jnp.int32), pltpu.SemaphoreType.DMA((3,))],
        "middle",
    )(held(tile_slot), held(tile_offset), held(slot_block), half, other, design, sources, obs_knot, att)
    pieces = call(
        later_sources,
        piece,
        [HBM] + [VMEM] * 3,
        [acc, pltpu.SMEM((tiles,), jnp.int32), pltpu.SemaphoreType.DMA((1,))],
        "later_sources",
    )(held(tile_slot), sources, y, numbers)
    own, att = att_sums(own, rims)
    half, other, names = src_sums(pieces, names, own)
    w_att, w_src, row = call(
        functools.partial(last_kernel, copies),
        (true, mine, f32(devices, 1, LANES)),
        [HBM] * 3 + [VMEM] * 10,
        [dense, knots, pltpu.VMEM((tiles, LANES), F32)]
        + [pltpu.SMEM((tiles,), jnp.int32)] * 2
        + [pltpu.SMEM(slot_block.shape, jnp.int32), pltpu.SemaphoreType.DMA((3,))],
        "last",
    )(
        held(tile_slot), held(tile_offset), held(slot_block), half, other, design, sources, obs_knot, y, numbers, z_att, z_src, att
    )
    row = lax.all_to_all(row, ("src", "tm"), 0, 0, tiled=True)
    src, att = call(
        final_kernel,
        (mine, f32(AXES, KN)),
        [VMEM] * 5,
        name="final",
    )(row, z_src, w_src, z_att, w_att)
    return jnp.transpose(src, (1, 0, 2)), att


def solution(mesh):
    placed = (
        P(("src", "tm"), None, None),
        P(("src", "tm"), None, None),
        P(("src", "tm"), None),
        P(("src", "tm"), None),
        P(("src", "tm"), None),
        P(("src", "tm")),
        P(("src", "tm")),
        P(("src", "tm")),
        P(("src", "tm"), None),
    )
    return jax.shard_map(
        shards,
        mesh=mesh,
        in_specs=placed,
        out_specs=(P(("src", "tm"), None, None), P(None, "tm")),
        check_vma=False,
    )
```
